256 devices in a mesh: aa: 16 (over z, x_lo), ba: 16 (over y, x_hi, core).
Axes of the slice: x: 4 (x_hi: 2, x_lo: 2; x = x_hi * 2 + x_lo), y: 4, z: 8, core: 2. Of those that a mesh axis runs over, the one named last changes fastest.
Arguments:
- b_vo: bfloat16 [128, 48, 4096], P('aa'), may hold values from -6 to 6
- b_vv: bfloat16 [16, 768, 4096], P('ba', None, 'aa'), may hold values from -0.09375 to 0.09375
- amplitudes: bfloat16 [768, 2304], P('ba'), may hold values from -0.21875 to 0.21875
- pair_amps: bfloat16 [128, 16, 2304], P('aa', 'ba'), may hold values from -0.875 to 0.875
- coulomb_occ: bfloat16 [48, 2304], replicated, may hold values from -6 to 6
- eps_occ: float32 [48], replicated, may hold values from -2 to -0.5
- eps_vir: float32 [768], replicated, may hold values from 0.2 to 3
- c_index: int32 [1], replicated, may hold values from 0 to 767
- a_index: int32 [128], P('aa'), may hold values from 0 to 767
- b_index: int32 [16], P('ba'), may hold values from 0 to 767
Outputs:
- gamma_vo: float32 [128, 48, 4096], P('aa', None, 'ba')
- vir_density: float32 [128, 8], P('aa')
The draws below stay inside these ranges and needn't reach their ends.
All inputs are finite; a program needn't handle non-finite values.
Results may differ from the reference program's by a relative error of at most 0.0026.
Values may be sent and summed in bfloat16 or wider, within the bound.
No kernel may reach another device: no remote copies, remote signals or barrier semaphores. Data moves between devices by JAX's collectives and lax.ppermute only.
A program may use at most 64 MiB of HBM per device.

```python
import jax
import jax.numpy as jnp
from jax import lax

O = 48
V = 768
NAUX = 4096
NA = 8
OO = 2304
VA = 128
VB = 16
N_AA = 16


def set_ends(values, stream_key, smallest, largest):
    longest = values.shape.index(max(values.shape))
    spots = []
    for shift in (0, 1):
        where = [jax.random.randint(jax.random.fold_in(stream_key, axis), (), 0, length) for axis, length in enumerate(values.shape)]
        where[longest] = (where[longest] + shift) % values.shape[longest]
        spots.append(tuple(where))
    return values.at[spots[0]].set(smallest).at[spots[1]].set(largest)


def levels(own_key, extent, cuts, least, largest):
    def one(dim, shards_of):
        heights = jax.random.uniform(jax.random.fold_in(jax.random.fold_in(own_key, 6), dim), (shards_of,), jnp.float32, least / len(cuts), largest / len(cuts))
        return jnp.repeat(jnp.exp(heights), extent[dim] // shards_of).reshape((-1,) + (1,) * (len(extent) - dim - 1))

    factor_of = one(*cuts[0])
    for cut in cuts[1:]:
        factor_of = factor_of * one(*cut)
    return factor_of


def noise(rng, dims, width, most, cuts=(), kind=jnp.bfloat16):
    factor_of = levels(rng, dims, cuts, -0.22, 0.18) if cuts else 1.0
    entries = jax.random.normal(rng, dims, jnp.float32) * width * factor_of
    return jnp.minimum(jnp.maximum(entries, -most), most).astype(kind)


def setup_inputs(seed: int = 0) -> dict:
    splits = jax.random.split(jax.random.key(seed), 11)
    b_vo = noise(splits[0], (VA, O, NAUX), 1.0, 6.0, ((0, 16),))
    b_vv = noise(splits[1], (VB, V, NAUX), NAUX ** -0.5, 0.09375, ((0, 16), (2, 16)))
    amplitudes = noise(splits[2], (V, OO), V ** -0.5, 0.21875, ((0, 16),))
    pair_amps = noise(splits[3], (VA, VB, OO), O ** -0.5, 0.875, ((0, 16), (1, 16)))
    coulomb_occ = noise(splits[4], (O, OO), 1.0, 6.0)
    eps_occ = jnp.clip(jax.random.uniform(splits[5], (O,), jnp.float32, -2.0, -0.5), -2.0, -0.5)
    eps_vir = jnp.clip(jax.random.uniform(splits[6], (V,), jnp.float32, 0.2, 3.0), 0.2, 3.0)
    c_index = jax.random.randint(splits[7], (1,), 0, V).astype(jnp.int32)
    a_index = set_ends(jax.random.randint(splits[8], (VA,), 0, V), jax.random.fold_in(splits[8], 1), 0, V - 1).astype(jnp.int32)
    b_index = set_ends(jax.random.randint(splits[9], (VB,), 0, V), jax.random.fold_in(splits[9], 1), 0, V - 1).astype(jnp.int32)
    return {"b_vo": b_vo, "b_vv": b_vv, "amplitudes": amplitudes, "pair_amps": pair_amps, "coulomb_occ": coulomb_occ, "eps_occ": eps_occ, "eps_vir": eps_vir, "c_index": c_index, "a_index": a_index, "b_index": b_index}


def contract_last(left, right):
    return lax.dot_general(left, right, (((1,), (1,)), ((), ())), preferred_element_type=jnp.float32)


def reference(b_vo, b_vv, amplitudes, pair_amps, coulomb_occ, eps_occ, eps_vir, c_index, a_index, b_index):
    vv_flat = b_vv.reshape(VB * V, NAUX)
    occ_three = (eps_occ[:, None, None] + eps_occ[None, :, None] + eps_occ[None, None, :]).reshape(O, OO)
    energy_b = eps_vir[b_index]
    energy_c = eps_vir[c_index[0]]

    def one_block(block):
        start = (block * NA).astype(jnp.int32)
        vo_block = lax.dynamic_slice_in_dim(b_vo, start, NA, 0)
        pair_block = lax.dynamic_slice_in_dim(pair_amps, start, NA, 0)
        energy_a = eps_vir[lax.dynamic_slice_in_dim(a_index, start, NA, 0)]
        integrals = contract_last(vo_block.reshape(NA * O, NAUX), vv_flat).astype(jnp.bfloat16)
        x_rows = integrals.reshape(NA, O, VB, V).transpose(0, 2, 1, 3).reshape(NA * VB * O, V)
        particle = jnp.dot(x_rows, amplitudes, preferred_element_type=jnp.float32)
        hole_term = jnp.dot(pair_block.reshape(NA * VB * O, O), coulomb_occ, preferred_element_type=jnp.float32)
        triples = (particle - hole_term).reshape(NA, VB, O, OO)
        denom = occ_three[None, None] - energy_a[:, None, None, None] - energy_b[None, :, None, None] - energy_c
        ratio = (triples / denom).astype(jnp.bfloat16)
        ratio_wide = ratio.astype(jnp.float32)
        density = jnp.einsum("abiq,cbiq->ac", ratio_wide, ratio_wide) / (VB * O * O)
        left = contract_last(ratio.reshape(NA * VB * O, OO), amplitudes).astype(jnp.bfloat16)
        left = left.reshape(NA, VB, O, V).transpose(0, 2, 1, 3).reshape(NA * O, VB * V)
        gamma = jnp.dot(left, vv_flat, preferred_element_type=jnp.float32).reshape(NA, O, NAUX)
        return gamma, density

    gamma, density = lax.map(one_block, jnp.arange(N_AA, dtype=jnp.int32))
    return gamma.reshape(VA, O, NAUX), density.reshape(VA, NA)
```

```python
import functools

import jax
import jax.numpy as jnp
from jax import lax
from jax.experimental import pallas as pl
from jax.experimental.pallas import tpu as pltpu
from jax.sharding import PartitionSpec as P

NZ = 8
NY = 4
RANKS = 16
VMEM_LIMIT = 52 * 1024 * 1024
TILE = 768
NT = (((1,), (1,)), ((), ()))


def shift_perm(step):
    return [(i, (i + step) % RANKS) for i in range(RANKS)]


def swap_perm(bit):
    return [(i, i ^ bit) for i in range(RANKS)]


def along_z(x, step):
    return lax.ppermute(x, "aa", shift_perm(2 * step))


def swap_x_lo(x):
    return lax.ppermute(x, "aa", swap_perm(1))


def along_y(x, step):
    return lax.ppermute(x, "ba", shift_perm(4 * step))


def swap_x_hi(x):
    return lax.ppermute(x, "ba", swap_perm(2))


def swap_core(x):
    return lax.ppermute(x, "ba", swap_perm(1))


def together(*arrays):
    return lax.optimization_barrier(arrays)


VMEM = pl.BlockSpec(memory_space=pltpu.VMEM)
SMEM = pl.BlockSpec(memory_space=pltpu.SMEM)
HBM = pl.BlockSpec(memory_space=pltpu.HBM)


def where_am_i():
    aa, ba = lax.axis_index("aa"), lax.axis_index("ba")
    z, x_lo = aa // 2, aa % 2
    y, x_hi, core = ba // 4, (ba // 2) % 2, ba % 2
    return z, x_lo, y, x_hi, core


def column_start(place, width):
    z, x_lo = where_am_i()[:2]
    column = (z + place % NZ) % NZ * 2 + (x_lo if place < NZ else 1 - x_lo)
    return pl.multiple_of(column * width, width)


def fetch(pairs, sems):
    copies = [pltpu.make_async_copy(*pair, sems.at[n]) for n, pair in enumerate(pairs)]
    for copy in copies:
        copy.start()
    return copies


def fetch_columns(places, a_ref, a_buf, sems):
    width = a_buf.shape[2]
    columns = [pl.ds(column_start(place, width), width) for place in places]
    return fetch([(a_ref.at[:, c], a_buf.at[n]) for n, c in enumerate(columns)], sems)


def terms_kernel(a_index_ref, b_index_ref, c_index_ref, table_ref, eps_ref, row_ref, col_ref):
    occupied = eps_ref.shape[1]
    along = lambda axis, shape: lax.broadcasted_iota(jnp.int32, shape, axis)
    square = (occupied, occupied)
    eps = jnp.sum(
        jnp.where(along(0, square) == along(1, square), eps_ref[...], 0.0), axis=1, keepdims=True
    )
    energy_b, energy_c = table_ref[b_index_ref[0]], table_ref[c_index_ref[0]]
    for n in range(a_index_ref.shape[0]):
        row_ref[n * occupied : (n + 1) * occupied] = (
            eps - table_ref[a_index_ref[n]] - energy_b - energy_c
        )
    wide = (occupied, col_ref.shape[1])
    picked = lambda labels: jnp.sum(
        jnp.where(along(0, wide) == labels, eps, 0.0), axis=0, keepdims=True
    )
    col_ref[...] = picked(along(1, wide) // occupied) + picked(along(1, wide) % occupied)


def energy_terms(tables):
    occupied = tables[-1].shape[1]
    return pl.pallas_call(
        terms_kernel,
        out_shape=(
            jax.ShapeDtypeStruct((tables[0].shape[0] * occupied, 1), jnp.float32),
            jax.ShapeDtypeStruct((1, occupied * occupied), jnp.float32),
        ),
        in_specs=[SMEM] * 4 + [VMEM],
        out_specs=(VMEM, VMEM),
        compiler_params=pltpu.CompilerParams(vmem_limit_bytes=VMEM_LIMIT),
    )(*tables)


def add_kernel(places, first, a_ref, *refs):
    count = len(places)
    pieces, rest = refs[:count], refs[count:]
    if not first:
        before_ref, rest = rest[0], rest[2:]
    out_ref, stack_ref, a_buf, a_sems, p_buf, p_sems, sems = rest
    copies = fetch_columns(places, a_ref, a_buf, a_sems)
    loads = fetch([(piece, p_buf.at[n]) for n, piece in enumerate(pieces)], p_sems)
    stores = []
    for n, place in enumerate(places):
        loads[n].wait()
        store = pltpu.make_async_copy(p_buf.at[n], stack_ref.at[place], sems.at[n])
        store.start()
        stores.append(store)
        copies[n].wait()
        terms = lax.dot_general(a_buf[n], p_buf[n], NT, preferred_element_type=jnp.float32)
        if n:
            out_ref[...] += terms
        else:
            out_ref[...] = terms if first else before_ref[...] + terms
    for store in stores:
        store.wait()


def add_products(places, pieces, a, before):
    rows = a.shape[0]
    virtuals, width = pieces[0].shape
    first = before is None
    count = len(pieces)
    return pl.pallas_call(
        functools.partial(add_kernel, places, first),
        out_shape=(
            jax.ShapeDtypeStruct((rows, virtuals), jnp.float32),
            jax.ShapeDtypeStruct((2 * NZ, virtuals, width), pieces[0].dtype),
        ),
        in_specs=[HBM] * (1 + count) + ([] if first else [VMEM, HBM]),
        out_specs=(VMEM, HBM),
        scratch_shapes=[
            pltpu.VMEM((count, rows, width), a.dtype),
            pltpu.SemaphoreType.DMA((count,)),
            pltpu.VMEM((count, virtuals, width), a.dtype),
            pltpu.SemaphoreType.DMA((count,)),
            pltpu.SemaphoreType.DMA((count,)),
        ],
        input_output_aliases={} if first else {2 + count: 1},
        compiler_params=pltpu.CompilerParams(vmem_limit_bytes=VMEM_LIMIT),
        cost_estimate=pl.CostEstimate(
            flops=2 * rows * virtuals * width * count,
            bytes_accessed=2 * virtuals * width * count,
            transcendentals=0,
        ),
    )(a, *pieces, *([] if first else before))


def gather_pieces(piece, amplitudes, pair_rows, a, tables):
    own, other = {0: piece}, {}
    get = lambda n: other[n - NZ] if n >= NZ else own[n]
    add = lambda places, before=None: add_products(places, [get(n) for n in places], a, before)
    own[7], own[1], other[0], amp_hi = together(
        along_z(piece, 1), along_z(piece, -1), swap_x_lo(piece), swap_x_hi(amplitudes)
    )
    amp_own = lax.all_gather(
        jnp.stack([amplitudes, amp_hi]),
        "ba",
        axis=0,
        axis_index_groups=[[n + 4 * m for m in range(NY)] for n in range(4)],
    )
    sums = add([0, 1, 7, NZ])
    own[6], own[2], other[1], sums, pair_rows = together(
        along_z(own[7], 1), along_z(own[1], -1), swap_x_lo(own[1]), sums, pair_rows
    )
    sums = add([2, 6, NZ + 1], sums)
    own[5], own[3], other[7], sums, terms = together(
        along_z(own[6], 1), along_z(own[2], -1), swap_x_lo(own[7]), sums, energy_terms(tables)
    )
    sums = add([3, 5, NZ + 7], sums)
    own[4], other[2], other[3], sums, amp_own = together(
        along_z(own[5], 1), along_z(other[1], -1), swap_x_lo(own[3]), sums, amp_own
    )
    amp_other = swap_core(amp_own)
    other[6], other[4], other[5] = (
        along_z(other[7], 1), along_z(other[3], -1), swap_x_lo(own[5])
    )
    sums, stack = add([4, NZ + 2, NZ + 3], sums)
    late = [NZ + 4, NZ + 5, NZ + 6]
    return late, [get(n) for n in late], sums, stack, terms, pair_rows, amp_own, amp_other


def chosen_copies(goes, passed, stack_ref, buf, sems):
    z, x_lo, _, x_hi, core = where_am_i()
    first = jnp.where(x_lo == core, goes, 1 - goes) * NZ + (z + x_hi + passed) % 2
    return [
        pltpu.make_async_copy(stack_ref.at[first + 2 * j], buf.at[j], sems.at[j]) for j in range(NY)
    ]


def gamma_dots(left, waits, buf, out_ref):
    rows = left.shape[0]
    for j in range(NY):
        waits[j].wait()
        out_ref[j * rows : (j + 1) * rows] = jnp.dot(
            left, buf[j], preferred_element_type=jnp.float32
        )


def middle_kernel(late, a_ref, *refs):
    count = len(late)
    pieces, (before_ref, row_ref, col_ref, pair_ref, coulomb_ref), rest = (
        refs[:count], refs[count : count + 5], refs[count + 5 :]
    )
    amp_own_ref, amp_other_ref, _, stack_ref, left_ref, keep_ref, sent_ref, *rest = rest
    a_buf, a_sems, p_buf, p_sems, sems, total, gram = rest[:7]
    keep_buf, keep_sems, sent_buf, sent_sems, amp_ref, amp_sems = rest[7:]
    a_copies = fetch_columns(late, a_ref, a_buf, a_sems)
    loads = fetch([(piece, p_buf.at[n]) for n, piece in enumerate(pieces)], p_sems)
    _, _, _, x_hi, core = where_am_i()
    part = amp_own_ref.shape[2]
    amp_copies = []
    for n in range(NY):
        for other_hi in range(2):
            for other_core, ref in enumerate((amp_own_ref, amp_other_ref)):
                hi = 1 - x_hi if other_hi else x_hi
                owner = (n * 2 + hi) * 2 + (1 - core if other_core else core)
                target = amp_ref.at[pl.ds(pl.multiple_of(owner * part, part), part)]
                amp_copies.append((ref.at[n, other_hi], target))
    amp_copies = fetch(amp_copies, amp_sems)
    stores = []
    products = before_ref[...]
    for n, place in enumerate(late):
        loads[n].wait()
        store = pltpu.make_async_copy(p_buf.at[n], stack_ref.at[place], sems.at[n])
        store.start()
        stores.append(store)
        a_copies[n].wait()
        products += lax.dot_general(a_buf[n], p_buf[n], NT, preferred_element_type=jnp.float32)
    x = products.astype(jnp.bfloat16)
    for store in stores:
        store.wait()
    sent_copies = chosen_copies(1, 1, stack_ref, sent_buf, sent_sems)
    keep_copies = chosen_copies(0, 1, stack_ref, keep_buf, keep_sems)
    for copy in amp_copies:
        copy.wait()
    for copy in sent_copies + keep_copies:
        copy.start()
    tiles = [slice(n, n + TILE) for n in range(0, amp_ref.shape[1], TILE)]
    for n, tile in enumerate(tiles):
        triples = jnp.dot(
            x, amp_ref[:, tile], preferred_element_type=jnp.float32
        ) - jnp.dot(pair_ref[...], coulomb_ref[:, tile], preferred_element_type=jnp.float32)
        ratio = (triples / (row_ref[...] + col_ref[:, tile])).astype(jnp.bfloat16)
        terms = lax.dot_general(ratio, amp_ref[:, tile], NT, preferred_element_type=jnp.float32)
        pairs = lax.dot_general(ratio, ratio, NT, preferred_element_type=jnp.float32)
        if n == 0:
            total[...] = terms
            gram[...] = pairs
        else:
            total[...] += terms
            gram[...] += pairs
    left_ref[...] = total[...].astype(left_ref.dtype)

    gamma_dots(left_ref[...], sent_copies, sent_buf, sent_ref)
    gamma_dots(left_ref[...], keep_copies, keep_buf, keep_ref)

    rows, occupied = pair_ref.shape
    width = keep_ref.shape[1]
    count = rows // occupied
    block = (occupied, rows)
    same = lax.broadcasted_iota(jnp.int32, block, 0) == lax.broadcasted_iota(jnp.int32, block, 1) % occupied
    picked = jnp.concatenate(
        [
            jnp.where(same, gram[n * occupied : (n + 1) * occupied], 0.0).sum(0, keepdims=True)
            for n in range(count)
        ]
    )
    owner = lax.broadcasted_iota(jnp.int32, (rows, width), 0) // occupied
    place = lax.broadcasted_iota(jnp.int32, (rows, width), 1)
    density = jnp.dot(
        picked,
        jnp.where(owner == place, 1.0, 0.0),
        precision=lax.Precision.HIGHEST,
        preferred_element_type=jnp.float32,
    )
    for out_ref in (keep_ref, sent_ref):
        out_ref[NY * rows : NY * rows + count] = density
        out_ref[NY * rows + count :] = jnp.zeros((16 - count, width), jnp.float32)


def middle(late, pieces, a, sums, stack, terms, pair_rows, coulomb, amp_own, amp_other):
    rows, virtuals = sums.shape
    width = pieces[0].shape[1]
    pair_cols = coulomb.shape[1]
    count = len(late)
    block = jax.ShapeDtypeStruct((NY * rows + 16, width), jnp.float32)
    buf = pltpu.VMEM((NY, virtuals, width), jnp.bfloat16)
    return pl.pallas_call(
        functools.partial(middle_kernel, late),
        out_shape=(
            jax.ShapeDtypeStruct(stack.shape, stack.dtype),
            jax.ShapeDtypeStruct((rows, virtuals), jnp.bfloat16),
            block,
            block,
        ),
        in_specs=[HBM] * (1 + count) + [VMEM] * 5 + [HBM] * 3,
        out_specs=(HBM, VMEM, VMEM, VMEM),
        scratch_shapes=[
            pltpu.VMEM((count, rows, width), a.dtype),
            pltpu.SemaphoreType.DMA((count,)),
            pltpu.VMEM((count, virtuals, width), a.dtype),
            pltpu.SemaphoreType.DMA((count,)),
            pltpu.SemaphoreType.DMA((count,)),
            pltpu.VMEM((rows, virtuals), jnp.float32),
            pltpu.VMEM((rows, rows), jnp.float32),
            buf,
            pltpu.SemaphoreType.DMA((NY,)),
            buf,
            pltpu.SemaphoreType.DMA((NY,)),
            pltpu.VMEM((virtuals, pair_cols), jnp.bfloat16),
            pltpu.SemaphoreType.DMA((RANKS,)),
        ],
        input_output_aliases={1 + count + 7: 0},
        compiler_params=pltpu.CompilerParams(vmem_limit_bytes=VMEM_LIMIT),
    )(a, *pieces, sums, *terms, pair_rows, coulomb, amp_own, amp_other, stack)


def rest_kernel(left_ref, stack_ref, keep_ref, sent_ref, keep_buf, keep_sems, sent_buf, sent_sems):
    sent_copies = chosen_copies(1, 0, stack_ref, sent_buf, sent_sems)
    keep_copies = chosen_copies(0, 0, stack_ref, keep_buf, keep_sems)
    for copy in sent_copies + keep_copies:
        copy.start()
    gamma_dots(left_ref[...], sent_copies, sent_buf, sent_ref)
    gamma_dots(left_ref[...], keep_copies, keep_buf, keep_ref)


def gamma_rest(left, stack):
    rows, virtuals = left.shape
    width = stack.shape[2]
    block = jax.ShapeDtypeStruct((NY * rows, width), jnp.float32)
    buf = pltpu.VMEM((NY, virtuals, width), jnp.bfloat16)
    return pl.pallas_call(
        rest_kernel,
        out_shape=(block, block),
        in_specs=[VMEM, HBM],
        out_specs=(VMEM, VMEM),
        scratch_shapes=[buf, pltpu.SemaphoreType.DMA((NY,))] * 2,
        compiler_params=pltpu.CompilerParams(vmem_limit_bytes=VMEM_LIMIT),
        cost_estimate=pl.CostEstimate(
            flops=4 * rows * virtuals * width * NY,
            bytes_accessed=4 * virtuals * width * NY,
            transcendentals=0,
        ),
    )(left, stack)


def two_parts(values):
    high = values.astype(jnp.bfloat16)
    return high, (values - high.astype(jnp.float32)).astype(jnp.bfloat16)


def route_kernel(with_density, kept_ref, recv_ref, mine_ref, *refs):
    messages = refs[:3]
    rows = mine_ref.shape[0]
    z, _, y, x_hi, _ = where_am_i()
    odd = (z + x_hi + with_density) % 2
    for j in range(NY):
        away = ((z + 2 * j + odd) % NZ // 2 - y + NY) % NY
        part = slice(j * rows, (j + 1) * rows)
        terms = kept_ref[part] + recv_ref[part]
        for n, ref in enumerate((mine_ref, *messages)):
            @pl.when(away == n)
            def _():
                ref[:rows] = terms.astype(ref.dtype)

    if with_density:
        density = kept_ref[NY * rows :] + recv_ref[NY * rows :]
        refs[3][...] = density
        high, low = two_parts(density)
        for ref in messages:
            ref[rows : rows + 16] = high
            ref[rows + 16 :] = low


def route(rows, kept, received, with_density):
    width = kept.shape[1]
    message = jax.ShapeDtypeStruct((rows + 32 * with_density, width), jnp.bfloat16)
    out = [jax.ShapeDtypeStruct((rows, width), jnp.float32)] + [message] * 3
    if with_density:
        out.append(jax.ShapeDtypeStruct((16, width), jnp.float32))
    return pl.pallas_call(
        functools.partial(route_kernel, with_density),
        out_shape=out,
        in_specs=[VMEM, VMEM],
        out_specs=[VMEM] * len(out),
        compiler_params=pltpu.CompilerParams(vmem_limit_bytes=VMEM_LIMIT),
    )(kept, received)


def wide(ref, first, rows):
    return ref[first : first + rows].astype(jnp.float32)


def passed_kernel(mine_ref, density_ref, a_ref, b_ref, c_ref, send_ref, kept_ref):
    rows = mine_ref.shape[0]
    arrived = (a_ref, b_ref, c_ref)
    total = mine_ref[...] + sum(wide(ref, 0, rows) for ref in arrived)
    send_ref[:rows] = total.astype(send_ref.dtype)
    density = density_ref[...]
    for ref in arrived:
        density += wide(ref, rows, 16) + wide(ref, rows + 16, 16)
    kept_ref[...] = density
    high, low = two_parts(density)
    send_ref[rows : rows + 16] = high
    send_ref[rows + 16 :] = low


def passed_sum(mine, density, arrived):
    rows, width = mine.shape
    return pl.pallas_call(
        passed_kernel,
        out_shape=(
            jax.ShapeDtypeStruct((rows + 32, width), jnp.bfloat16),
            jax.ShapeDtypeStruct(density.shape, jnp.float32),
        ),
        in_specs=[VMEM] * 5,
        out_specs=(VMEM,) * 2,
        compiler_params=pltpu.CompilerParams(vmem_limit_bytes=VMEM_LIMIT),
    )(mine, density, *arrived)


def last_kernel(scale, mine_ref, a_ref, b_ref, c_ref, density_ref, recv_ref, gamma_ref, out_ref):
    rows = mine_ref.shape[0]
    total = mine_ref[...] + sum(wide(ref, 0, rows) for ref in (a_ref, b_ref, c_ref))
    gamma_ref[...] = total + wide(recv_ref, 0, rows)
    arrived = wide(recv_ref, rows, 16) + wide(recv_ref, rows + 16, 16)
    out_ref[...] = (density_ref[...] + arrived) / scale


def last_sum(scale, mine, arrived, density, received):
    return pl.pallas_call(
        functools.partial(last_kernel, scale),
        out_shape=(
            jax.ShapeDtypeStruct(mine.shape, jnp.float32),
            jax.ShapeDtypeStruct(density.shape, jnp.float32),
        ),
        in_specs=[VMEM] * 6,
        out_specs=(VMEM, VMEM),
        compiler_params=pltpu.CompilerParams(vmem_limit_bytes=VMEM_LIMIT),
    )(mine, *arrived, density, received)


def to_owners(messages):
    one, two, three = messages
    return along_y(one, 1), along_y(two, 2), along_y(three, -1)


def body(
    b_vo, b_vv, amplitudes, pair_amps, coulomb_occ, eps_occ, eps_vir, c_index, a_index, b_index
):
    count_a, occupied, aux_all = b_vo.shape
    rows = count_a * occupied
    virtuals = b_vv.shape[1]
    pair_cols = amplitudes.shape[1]
    vo_rows = b_vo.reshape(rows, aux_all)
    tables = (a_index, b_index, c_index, eps_vir, eps_occ.reshape(1, occupied))
    late, pieces, sums, stack, terms, pair_rows, amp_own, amp_other = gather_pieces(
        b_vv[0], amplitudes, pair_amps.reshape(rows, occupied), vo_rows, tables
    )
    stack, left, keep_b, sent_b = middle(
        late, pieces, vo_rows, sums, stack, terms, pair_rows, coulomb_occ, amp_own, amp_other
    )
    came_b, left = together(swap_core(sent_b), left)
    keep_a, sent_a = gamma_rest(left, stack)
    came_a = swap_core(sent_a)
    mine, *messages, density = route(rows, keep_b, came_b, True)
    arrived = to_owners(messages)
    mine_keep, *messages = route(rows, keep_a, came_a, False)
    arrived_keep = to_owners(messages)
    send, density = passed_sum(mine, density, arrived)
    scale = lax.axis_size("ba") * occupied * occupied
    gamma, density = last_sum(scale, mine_keep, arrived_keep, density, swap_x_hi(send))
    return gamma.reshape(count_a, occupied, gamma.shape[1]), density[:count_a, :count_a]


def solution(mesh):
    placed = (
        P("aa", None, None),
        P("ba", None, "aa"),
        P("ba", None),
        P("aa", "ba", None),
        P(),
        P(),
        P(),
        P(),
        P("aa"),
        P("ba"),
    )
    return jax.shard_map(
        body,
        mesh=mesh,
        in_specs=placed,
        out_specs=(P("aa", None, "ba"), P("aa", None)),
        check_vma=False,
    )
```

```python
import functools

import jax
import jax.numpy as jnp
from jax import lax
from jax.experimental import pallas as pl
from jax.experimental.pallas import tpu as pltpu
from jax.sharding import PartitionSpec as P

NZ = 8
NY = 4
RANKS = 16
VMEM_LIMIT = 24 * 1024 * 1024
SMALL_LIMIT = 16 * 1024 * 1024
TILE = 768
NT = (((1,), (1,)), ((), ()))


def shift_perm(step):
    return [(i, (i + step) % RANKS) for i in range(RANKS)]


def swap_perm(bit):
    return [(i, i ^ bit) for i in range(RANKS)]


def along_z(x, step):
    return lax.ppermute(x, "aa", shift_perm(2 * step))


def swap_x_lo(x):
    return lax.ppermute(x, "aa", swap_perm(1))


def along_y(x, step):
    return lax.ppermute(x, "ba", shift_perm(4 * step))


def swap_x_hi(x):
    return lax.ppermute(x, "ba", swap_perm(2))


def swap_core(x):
    return lax.ppermute(x, "ba", swap_perm(1))


def together(*arrays):
    return lax.optimization_barrier(arrays)


VMEM = pl.BlockSpec(memory_space=pltpu.VMEM)
SMEM = pl.BlockSpec(memory_space=pltpu.SMEM)


def where_am_i():
    aa, ba = lax.axis_index("aa"), lax.axis_index("ba")
    z, x_lo = aa // 2, aa % 2
    y, x_hi, core = ba // 4, (ba // 2) % 2, ba % 2
    return z, x_lo, y, x_hi, core


def column_start(place, width):
    z, x_lo = where_am_i()[:2]
    column = (z + place % NZ) % NZ * 2 + (x_lo if place < NZ else 1 - x_lo)
    return pl.multiple_of(column * width, width)


def columns_of(a_ref, place, width):
    return a_ref[:, pl.ds(column_start(place, width), width)]


def terms_kernel(a_index_ref, b_index_ref, c_index_ref, table_ref, eps_ref, row_ref, col_ref):
    occupied = eps_ref.shape[1]
    along = lambda axis, shape: lax.broadcasted_iota(jnp.int32, shape, axis)
    square = (occupied, occupied)
    eps = jnp.sum(
        jnp.where(along(0, square) == along(1, square), eps_ref[...], 0.0), axis=1, keepdims=True
    )
    energy_b, energy_c = table_ref[b_index_ref[0]], table_ref[c_index_ref[0]]
    for n in range(a_index_ref.shape[0]):
        row_ref[n * occupied : (n + 1) * occupied] = (
            eps - table_ref[a_index_ref[n]] - energy_b - energy_c
        )
    wide = (occupied, col_ref.shape[1])
    picked = lambda labels: jnp.sum(
        jnp.where(along(0, wide) == labels, eps, 0.0), axis=0, keepdims=True
    )
    col_ref[...] = picked(along(1, wide) // occupied) + picked(along(1, wide) % occupied)


def energy_terms(tables):
    occupied = tables[-1].shape[1]
    return pl.pallas_call(
        terms_kernel,
        out_shape=(
            jax.ShapeDtypeStruct((tables[0].shape[0] * occupied, 1), jnp.float32),
            jax.ShapeDtypeStruct((1, occupied * occupied), jnp.float32),
        ),
        in_specs=[SMEM] * 4 + [VMEM],
        out_specs=(VMEM, VMEM),
        compiler_params=pltpu.CompilerParams(vmem_limit_bytes=SMALL_LIMIT),
    )(*tables)


def pack_kernel(*refs):
    for n, ref in enumerate(refs[:-1]):
        refs[-1][n] = ref[...]


def pack(arrays):
    return pl.pallas_call(
        pack_kernel,
        out_shape=jax.ShapeDtypeStruct((len(arrays), *arrays[0].shape), arrays[0].dtype),
        in_specs=[VMEM] * len(arrays),
        out_specs=VMEM,
        compiler_params=pltpu.CompilerParams(vmem_limit_bytes=SMALL_LIMIT),
    )(*arrays)


def add_kernel(places, first, a_ref, *refs):
    count = len(places)
    pieces, rest = refs[:count], refs[count:]
    if first:
        out_ref, stack_ref = rest
    else:
        before_ref, _, out_ref, stack_ref = rest
    for n, (place, piece) in enumerate(zip(places, pieces)):
        stack_ref[place] = piece[...]
        terms = lax.dot_general(
            columns_of(a_ref, place, piece.shape[1]),
            piece[...],
            NT,
            preferred_element_type=jnp.float32,
        )
        if n:
            out_ref[...] += terms
        else:
            out_ref[...] = terms if first else before_ref[...] + terms


def add_products(places, pieces, a, before=()):
    rows = a.shape[0]
    virtuals, width = pieces[0].shape
    count = len(pieces)
    return pl.pallas_call(
        functools.partial(add_kernel, places, not before),
        out_shape=(
            jax.ShapeDtypeStruct((rows, virtuals), jnp.float32),
            jax.ShapeDtypeStruct((2 * NZ, virtuals, width), pieces[0].dtype),
        ),
        in_specs=[VMEM] * (1 + count + len(before)),
        out_specs=(VMEM, VMEM),
        input_output_aliases={1 + count: 0, 2 + count: 1} if before else {},
        compiler_params=pltpu.CompilerParams(vmem_limit_bytes=VMEM_LIMIT),
        cost_estimate=pl.CostEstimate(
            flops=2 * rows * virtuals * width * count,
            bytes_accessed=2 * virtuals * width * count,
            transcendentals=0,
        ),
    )(a, *pieces, *before)


def gather_pieces(piece, amplitudes, pair_rows, a, tables):
    own, other = {0: piece}, {}
    get = lambda n: other[n - NZ] if n >= NZ else own[n]
    add = lambda places, **rest: add_products(places, [get(n) for n in places], a, **rest)
    own[7], own[1], other[0], amp_hi, terms, pair_rows = together(
        along_z(piece, 1),
        along_z(piece, -1),
        swap_x_lo(piece),
        swap_x_hi(amplitudes),
        energy_terms(tables),
        pair_rows,
    )
    amp = pack([amplitudes, amp_hi])
    sums = add([0, 1, 7, NZ])
    own[6], own[2], other[1], sums, amp_up, amp_down = together(
        along_z(own[7], 1),
        along_z(own[1], -1),
        swap_x_lo(own[1]),
        sums,
        along_y(amp, -1),
        along_y(amp, 1),
    )
    sums = add([2, 6, NZ + 1], before=sums)
    own[5], own[3], other[7], sums, amp_far = together(
        along_z(own[6], 1), along_z(own[2], -1), swap_x_lo(own[7]), sums, along_y(amp_up, -1)
    )
    amp_own = pack([amp, amp_up, amp_far, amp_down])
    sums = add([3, 5, NZ + 7], before=sums)
    own[4], other[2], other[3], sums, amp_other = together(
        along_z(own[5], 1), along_z(other[1], -1), swap_x_lo(own[3]), sums, swap_core(amp_own)
    )
    other[6], other[4], other[5] = (
        along_z(other[7], 1), along_z(other[3], -1), swap_x_lo(own[5])
    )
    sums, stack = add([4, NZ + 2, NZ + 3], before=sums)
    late = [NZ + 4, NZ + 5, NZ + 6]
    return late, [get(n) for n in late], sums, stack, terms, pair_rows, amp_own, amp_other


def gamma_dots(goes, left, stack_ref, out_ref):
    z, x_lo, y, x_hi, core = where_am_i()
    first = jnp.where(x_lo == core, goes, 1 - goes) * NZ
    rows = left.shape[0]
    for n in range(NZ):
        target = (y + n) % NY * 2 + (x_hi if n < NY else 1 - x_hi)
        out_ref[n * rows : (n + 1) * rows] = jnp.dot(
            left, stack_ref[first + (target - z + NZ) % NZ], preferred_element_type=jnp.float32
        ).astype(out_ref.dtype)


def middle_kernel(late, a_ref, *refs):
    count = len(late)
    pieces, (before_ref, row_ref, col_ref, pair_ref, coulomb_ref), rest = (
        refs[:count], refs[count : count + 5], refs[count + 5 :]
    )
    amp_refs, (_, stack_ref, keep_ref, sent_ref, *rest) = rest[:2], rest[2:]
    left_ref, total, gram, amp_ref = rest
    products = before_ref[...]
    for place, piece in zip(late, pieces):
        stack_ref[place] = piece[...]
        products += lax.dot_general(
            columns_of(a_ref, place, piece.shape[1]),
            piece[...],
            NT,
            preferred_element_type=jnp.float32,
        )
    x = products.astype(jnp.bfloat16)

    _, _, y, x_hi, core = where_am_i()
    part = amp_refs[0].shape[2]
    for other_core, ref in enumerate(amp_refs):
        for n in range(NY):
            for other_hi in range(2):
                hi = 1 - x_hi if other_hi else x_hi
                owner = ((y + n) % NY * 2 + hi) * 2 + (1 - core if other_core else core)
                target = pl.ds(pl.multiple_of(owner * part, part), part)
                amp_ref[target] = ref[n, other_hi]
    tiles = [slice(n, n + TILE) for n in range(0, amp_ref.shape[1], TILE)]
    for n, tile in enumerate(tiles):
        triples = jnp.dot(
            x, amp_ref[:, tile], preferred_element_type=jnp.float32
        ) - jnp.dot(pair_ref[...], coulomb_ref[:, tile], preferred_element_type=jnp.float32)
        ratio = (triples / (row_ref[...] + col_ref[:, tile])).astype(jnp.bfloat16)
        terms = lax.dot_general(ratio, amp_ref[:, tile], NT, preferred_element_type=jnp.float32)
        pairs = lax.dot_general(ratio, ratio, NT, preferred_element_type=jnp.float32)
        if n == 0:
            total[...] = terms
            gram[...] = pairs
        else:
            total[...] += terms
            gram[...] += pairs
    left_ref[...] = total[...].astype(left_ref.dtype)

    gamma_dots(1, left_ref[...], stack_ref, sent_ref)
    gamma_dots(0, left_ref[...], stack_ref, keep_ref)

    rows, occupied = pair_ref.shape
    width = keep_ref.shape[1]
    count = rows // occupied
    block = (occupied, rows)
    same = lax.broadcasted_iota(jnp.int32, block, 0) == lax.broadcasted_iota(jnp.int32, block, 1) % occupied
    picked = jnp.concatenate(
        [
            jnp.where(same, gram[n * occupied : (n + 1) * occupied], 0.0).sum(0, keepdims=True)
            for n in range(count)
        ]
    )
    owner = lax.broadcasted_iota(jnp.int32, (rows, width), 0) // occupied
    place = lax.broadcasted_iota(jnp.int32, (rows, width), 1)
    density = jnp.dot(
        picked,
        jnp.where(owner == place, 1.0, 0.0),
        precision=lax.Precision.HIGHEST,
        preferred_element_type=jnp.float32,
    )
    density = jnp.concatenate([density, jnp.zeros((16 - count, width), jnp.float32)])
    keep_ref[NZ * rows :] = density
    put_parts(sent_ref, NZ * rows, density)


def middle(late, pieces, a, sums, stack, terms, pair_rows, coulomb, amps):
    rows, virtuals = sums.shape
    width = pieces[0].shape[1]
    pair_cols = coulomb.shape[1]
    return pl.pallas_call(
        functools.partial(middle_kernel, late),
        out_shape=(
            jax.ShapeDtypeStruct(stack.shape, stack.dtype),
            jax.ShapeDtypeStruct((NZ * rows + 16, width), jnp.float32),
            jax.ShapeDtypeStruct((NZ * rows + 32, width), jnp.bfloat16),
        ),
        in_specs=[VMEM] * (7 + len(late) + len(amps)),
        out_specs=(VMEM,) * 3,
        input_output_aliases={6 + len(late) + len(amps): 0},
        scratch_shapes=[
            pltpu.VMEM((rows, virtuals), jnp.bfloat16),
            pltpu.VMEM((rows, virtuals), jnp.float32),
            pltpu.VMEM((rows, rows), jnp.float32),
            pltpu.VMEM((virtuals, pair_cols), jnp.bfloat16),
        ],
        compiler_params=pltpu.CompilerParams(vmem_limit_bytes=VMEM_LIMIT),
    )(a, *pieces, sums, *terms, pair_rows, coulomb, *amps, stack)


def put_parts(ref, first, values):
    high = values.astype(jnp.bfloat16)
    ref[first : first + 16] = high
    ref[first + 16 : first + 32] = (values - high.astype(jnp.float32)).astype(jnp.bfloat16)


def wide(ref, first, rows):
    return ref[first : first + rows].astype(jnp.float32)


def got_parts(ref, first):
    return wide(ref, first, 16) + wide(ref, first + 16, 16)


def first_kernel(kept_ref, recv_ref, mine_ref, one_ref, two_ref, three_ref, keep_ref, send_ref, out_ref):
    half = mine_ref.shape[0] // 2
    rows = 2 * half
    for hi in range(2):
        for n, ref in enumerate((mine_ref, one_ref, two_ref, three_ref)):
            first = (hi * NY + n) * rows
            upper = kept_ref[first : first + half] + wide(recv_ref, first, half)
            ref[hi * half : (hi + 1) * half] = upper.astype(ref.dtype)
            lower = kept_ref[first + half : first + rows] + wide(recv_ref, first + half, half)
            ref = send_ref if hi else keep_ref
            ref[n * half : (n + 1) * half] = lower.astype(ref.dtype)
    density = kept_ref[NZ * rows :] + got_parts(recv_ref, NZ * rows)
    out_ref[...] = density
    put_parts(send_ref, NY * half, density)


def first_sums(kept, received):
    rows, width = (kept.shape[0] - 16) // NZ, kept.shape[1]
    shape = lambda n, kind: jax.ShapeDtypeStruct((n, width), kind)
    message = shape(rows, jnp.bfloat16)
    return pl.pallas_call(
        first_kernel,
        out_shape=(
            shape(rows, jnp.float32),
            message,
            message,
            message,
            shape(NY * rows // 2, jnp.float32),
            shape(NY * rows // 2 + 32, jnp.bfloat16),
            shape(16, jnp.float32),
        ),
        in_specs=[VMEM] * 2,
        out_specs=(VMEM,) * 7,
        compiler_params=pltpu.CompilerParams(vmem_limit_bytes=SMALL_LIMIT),
    )(kept, received)


def second_kernel(
    mine_ref, a_ref, b_ref, c_ref, keep_ref, recv_ref, density_ref,
    upper_ref, send_ref, lower_ref, one_ref, two_ref, three_ref, out_ref,
):
    half = upper_ref.shape[0]
    for hi, ref in enumerate((upper_ref, send_ref)):
        first = hi * half
        arrived = sum(wide(other, first, half) for other in (a_ref, b_ref, c_ref))
        ref[...] = (mine_ref[first : first + half] + arrived).astype(ref.dtype)
    density = density_ref[...] + got_parts(recv_ref, NY * half)
    out_ref[...] = density
    for n, ref in enumerate((lower_ref, one_ref, two_ref, three_ref)):
        first = n * half
        total = keep_ref[first : first + half] + wide(recv_ref, first, half)
        ref[:half] = total.astype(ref.dtype)
        if n:
            put_parts(ref, half, density)


def second_sums(mine, arrived, keep, received, density):
    half, width = mine.shape[0] // 2, mine.shape[1]
    shape = lambda n, kind: jax.ShapeDtypeStruct((n, width), kind)
    message = shape(half + 32, jnp.bfloat16)
    return pl.pallas_call(
        second_kernel,
        out_shape=(
            shape(half, jnp.float32),
            shape(half, jnp.bfloat16),
            shape(half, jnp.float32),
            message,
            message,
            message,
            shape(16, jnp.float32),
        ),
        in_specs=[VMEM] * 7,
        out_specs=(VMEM,) * 7,
        compiler_params=pltpu.CompilerParams(vmem_limit_bytes=SMALL_LIMIT),
    )(mine, *arrived, keep, received, density)


def last_kernel(
    scale, upper_ref, recv_ref, lower_ref, a_ref, b_ref, c_ref, density_ref, gamma_ref, out_ref
):
    half = upper_ref.shape[0]
    gamma_ref[:half] = upper_ref[...] + wide(recv_ref, 0, half)
    arrived = (a_ref, b_ref, c_ref)
    gamma_ref[half:] = lower_ref[...] + sum(wide(ref, 0, half) for ref in arrived)
    density = density_ref[...] + sum(got_parts(ref, half) for ref in arrived)
    count = out_ref.shape[0]
    out_ref[...] = density[:count, :count] / scale


def last_sums(scale, count, upper, received, lower, arrived, density):
    half, width = upper.shape
    return pl.pallas_call(
        functools.partial(last_kernel, scale),
        out_shape=(
            jax.ShapeDtypeStruct((2 * half, width), jnp.float32),
            jax.ShapeDtypeStruct((count, count), jnp.float32),
        ),
        in_specs=[VMEM] * 7,
        out_specs=(VMEM, VMEM),
        compiler_params=pltpu.CompilerParams(vmem_limit_bytes=SMALL_LIMIT),
    )(upper, received, lower, *arrived, density)


def to_owners(messages):
    one, two, three = messages
    return along_y(one, 1), along_y(two, 2), along_y(three, -1)


def body(
    b_vo, b_vv, amplitudes, pair_amps, coulomb_occ, eps_occ, eps_vir, c_index, a_index, b_index
):
    count_a, occupied, aux_all = b_vo.shape
    rows = count_a * occupied
    virtuals = b_vv.shape[1]
    pair_cols = amplitudes.shape[1]
    vo_rows = b_vo.reshape(rows, aux_all)
    tables = (a_index, b_index, c_index, eps_vir, eps_occ.reshape(1, occupied))
    late, pieces, sums, stack, terms, pair_rows, *amps = gather_pieces(
        b_vv[0], amplitudes, pair_amps.reshape(rows, occupied), vo_rows, tables
    )
    _, kept, sent = middle(late, pieces, vo_rows, sums, stack, terms, pair_rows, coulomb_occ, amps)
    mine, *messages, keep, send, density = first_sums(kept, swap_core(sent))
    arrived, received = together(to_owners(messages), swap_x_hi(send))
    upper, send, lower, *messages, density = second_sums(mine, arrived, keep, received, density)
    arrived, received = together(to_owners(messages), swap_x_hi(send))
    scale = lax.axis_size("ba") * occupied * occupied
    gamma, density = last_sums(scale, count_a, upper, received, lower, arrived, density)
    return gamma.reshape(count_a, occupied, gamma.shape[1]), density


def solution(mesh):
    placed = (
        P("aa", None, None),
        P("ba", None, "aa"),
        P("ba", None),
        P("aa", "ba", None),
        P(),
        P(),
        P(),
        P(),
        P("aa"),
        P("ba"),
    )
    return jax.shard_map(
        body,
        mesh=mesh,
        in_specs=placed,
        out_specs=(P("aa", None, "ba"), P("aa", None)),
        check_vma=False,
    )
```

```python
import functools

import jax
import jax.numpy as jnp
from jax import lax
from jax.experimental import pallas as pl
from jax.experimental.pallas import tpu as pltpu
from jax.sharding import PartitionSpec as P

NZ = 8
NY = 4
RANKS = 16
VMEM_LIMIT = 24 * 1024 * 1024
SMALL_LIMIT = 16 * 1024 * 1024
TILE = 768
UPPER = 160
NT = (((1,), (1,)), ((), ()))


def shift_perm(step):
    return [(i, (i + step) % RANKS) for i in range(RANKS)]


def swap_perm(bit):
    return [(i, i ^ bit) for i in range(RANKS)]


def along_z(x, step):
    return lax.ppermute(x, "aa", shift_perm(2 * step))


def swap_x_lo(x):
    return lax.ppermute(x, "aa", swap_perm(1))


def along_y(x, step):
    return lax.ppermute(x, "ba", shift_perm(4 * step))


def swap_x_hi(x):
    return lax.ppermute(x, "ba", swap_perm(2))


def swap_core(x):
    return lax.ppermute(x, "ba", swap_perm(1))


def together(*arrays):
    return lax.optimization_barrier(arrays)


VMEM = pl.BlockSpec(memory_space=pltpu.VMEM)
SMEM = pl.BlockSpec(memory_space=pltpu.SMEM)


def where_am_i():
    aa, ba = lax.axis_index("aa"), lax.axis_index("ba")
    z, x_lo = aa // 2, aa % 2
    y, x_hi, core = ba // 4, (ba // 2) % 2, ba % 2
    return z, x_lo, y, x_hi, core


def column_start(place, width):
    z, x_lo = where_am_i()[:2]
    column = (z + place % NZ) % NZ * 2 + (x_lo if place < NZ else 1 - x_lo)
    return pl.multiple_of(column * width, width)


def columns_of(a_ref, place, width):
    return a_ref[:, pl.ds(column_start(place, width), width)]


def terms_kernel(a_index_ref, b_index_ref, c_index_ref, table_ref, eps_ref, row_ref, col_ref):
    occupied = eps_ref.shape[1]
    along = lambda axis, shape: lax.broadcasted_iota(jnp.int32, shape, axis)
    square = (occupied, occupied)
    eps = jnp.sum(
        jnp.where(along(0, square) == along(1, square), eps_ref[...], 0.0), axis=1, keepdims=True
    )
    energy_b, energy_c = table_ref[b_index_ref[0]], table_ref[c_index_ref[0]]
    for n in range(a_index_ref.shape[0]):
        row_ref[n * occupied : (n + 1) * occupied] = (
            eps - table_ref[a_index_ref[n]] - energy_b - energy_c
        )
    wide = (occupied, col_ref.shape[1])
    picked = lambda labels: jnp.sum(
        jnp.where(along(0, wide) == labels, eps, 0.0), axis=0, keepdims=True
    )
    col_ref[...] = picked(along(1, wide) // occupied) + picked(along(1, wide) % occupied)


def energy_terms(tables):
    occupied = tables[-1].shape[1]
    return pl.pallas_call(
        terms_kernel,
        out_shape=(
            jax.ShapeDtypeStruct((tables[0].shape[0] * occupied, 1), jnp.float32),
            jax.ShapeDtypeStruct((1, occupied * occupied), jnp.float32),
        ),
        in_specs=[SMEM] * 4 + [VMEM],
        out_specs=(VMEM, VMEM),
        compiler_params=pltpu.CompilerParams(vmem_limit_bytes=SMALL_LIMIT),
    )(*tables)


def pack_kernel(*refs):
    for n, ref in enumerate(refs[:-1]):
        refs[-1][n] = ref[...]


def pack(arrays):
    return pl.pallas_call(
        pack_kernel,
        out_shape=jax.ShapeDtypeStruct((len(arrays), *arrays[0].shape), arrays[0].dtype),
        in_specs=[VMEM] * len(arrays),
        out_specs=VMEM,
        compiler_params=pltpu.CompilerParams(vmem_limit_bytes=SMALL_LIMIT),
    )(*arrays)


def whole_kernel(own_ref, other_ref, out_ref):
    _, _, y, x_hi, core = where_am_i()
    part = own_ref.shape[2]
    for other_core, ref in enumerate((own_ref, other_ref)):
        for n in range(NY):
            for other_hi in range(2):
                hi = 1 - x_hi if other_hi else x_hi
                owner = ((y + n) % NY * 2 + hi) * 2 + (1 - core if other_core else core)
                out_ref[pl.ds(pl.multiple_of(owner * part, part), part)] = ref[n, other_hi]


def whole_amplitudes(own, other):
    part, columns = own.shape[2:]
    return pl.pallas_call(
        whole_kernel,
        out_shape=jax.ShapeDtypeStruct((RANKS * part, columns), own.dtype),
        in_specs=[VMEM] * 2,
        out_specs=VMEM,
        compiler_params=pltpu.CompilerParams(vmem_limit_bytes=SMALL_LIMIT),
    )(own, other)


def add_kernel(places, first, a_ref, *refs):
    count = len(places)
    pieces, rest = refs[:count], refs[count:]
    if first:
        out_ref, stack_ref = rest
    else:
        before_ref, _, out_ref, stack_ref = rest
    for n, (place, piece) in enumerate(zip(places, pieces)):
        stack_ref[place] = piece[...]
        terms = lax.dot_general(
            columns_of(a_ref, place, piece.shape[1]),
            piece[...],
            NT,
            preferred_element_type=jnp.float32,
        )
        if n:
            out_ref[...] += terms
        else:
            out_ref[...] = terms if first else before_ref[...] + terms


def add_products(places, pieces, a, before=()):
    rows = a.shape[0]
    virtuals, width = pieces[0].shape
    count = len(pieces)
    return pl.pallas_call(
        functools.partial(add_kernel, places, not before),
        out_shape=(
            jax.ShapeDtypeStruct((rows, virtuals), jnp.float32),
            jax.ShapeDtypeStruct((2 * NZ, virtuals, width), pieces[0].dtype),
        ),
        in_specs=[VMEM] * (1 + count + len(before)),
        out_specs=(VMEM, VMEM),
        input_output_aliases={1 + count: 0, 2 + count: 1} if before else {},
        compiler_params=pltpu.CompilerParams(vmem_limit_bytes=VMEM_LIMIT),
        cost_estimate=pl.CostEstimate(
            flops=2 * rows * virtuals * width * count,
            bytes_accessed=2 * virtuals * width * count,
            transcendentals=0,
        ),
    )(a, *pieces, *before)


def gather_pieces(piece, amplitudes, pair_rows, a, tables):
    own, other = {0: piece}, {}
    get = lambda n: other[n - NZ] if n >= NZ else own[n]
    add = lambda places, **rest: add_products(places, [get(n) for n in places], a, **rest)
    own[7], own[1], other[0], amp_hi, terms, pair_rows, sums = together(
        along_z(piece, 1),
        along_z(piece, -1),
        swap_x_lo(piece),
        swap_x_hi(amplitudes),
        energy_terms(tables),
        pair_rows,
        add([0]),
    )
    amp = pack([amplitudes, amp_hi])
    sums = add([1, 7, NZ], before=sums)
    amp_up, amp_down = along_y(amp, -1), along_y(amp, 1)
    own[6], own[2], other[1], sums = together(
        along_z(own[7], 1), along_z(own[1], -1), swap_x_lo(own[1]), sums
    )
    sums = add([2, 6, NZ + 1], before=sums)
    own[5], own[3], other[7], sums, amp_up, amp_down = together(
        along_z(own[6], 1), along_z(own[2], -1), swap_x_lo(own[7]), sums, amp_up, amp_down
    )
    sums = add([3, 5, NZ + 7], before=sums)
    own[4], other[2], other[3], sums, amp_far = together(
        along_z(own[5], 1), along_z(other[1], -1), swap_x_lo(own[3]), sums, along_y(amp_up, -1)
    )
    amp_own = pack([amp, amp_up, amp_far, amp_down])
    amp_other = swap_core(amp_own)
    other[6], other[4], other[5] = (
        along_z(other[7], 1), along_z(other[3], -1), swap_x_lo(own[5])
    )
    sums, stack = add([4, NZ + 2, NZ + 3], before=sums)
    late = [NZ + 4, NZ + 5, NZ + 6]
    return late, [get(n) for n in late], sums, stack, terms, pair_rows, whole_amplitudes(amp_own, amp_other)


def gamma_dots(goes, left, stack_ref, out_ref):
    z, x_lo, y, x_hi, core = where_am_i()
    first = jnp.where(x_lo == core, goes, 1 - goes) * NZ
    rows = left.shape[0]
    for n in range(NZ):
        target = (y + n) % NY * 2 + (x_hi if n < NY else 1 - x_hi)
        out_ref[n * rows : (n + 1) * rows] = jnp.dot(
            left, stack_ref[first + (target - z + NZ) % NZ], preferred_element_type=jnp.float32
        ).astype(out_ref.dtype)


def middle_kernel(late, a_ref, *refs):
    count = len(late)
    pieces, (before_ref, row_ref, col_ref, pair_ref, coulomb_ref), rest = (
        refs[:count], refs[count : count + 5], refs[count + 5 :]
    )
    amp_ref, _, stack_ref, left_ref, sent_ref, density_ref, total, gram = rest
    products = before_ref[...]
    for place, piece in zip(late, pieces):
        stack_ref[place] = piece[...]
        products += lax.dot_general(
            columns_of(a_ref, place, piece.shape[1]),
            piece[...],
            NT,
            preferred_element_type=jnp.float32,
        )
    x = products.astype(jnp.bfloat16)

    tiles = [slice(n, n + TILE) for n in range(0, amp_ref.shape[1], TILE)]
    for n, tile in enumerate(tiles):
        triples = jnp.dot(
            x, amp_ref[:, tile], preferred_element_type=jnp.float32
        ) - jnp.dot(pair_ref[...], coulomb_ref[:, tile], preferred_element_type=jnp.float32)
        ratio = (triples / (row_ref[...] + col_ref[:, tile])).astype(jnp.bfloat16)
        terms = lax.dot_general(ratio, amp_ref[:, tile], NT, preferred_element_type=jnp.float32)
        pairs = lax.dot_general(ratio, ratio, NT, preferred_element_type=jnp.float32)
        if n == 0:
            total[...] = terms
            gram[...] = pairs
        else:
            total[...] += terms
            gram[...] += pairs
    left_ref[...] = total[...].astype(left_ref.dtype)

    gamma_dots(1, left_ref[...], stack_ref, sent_ref)

    rows, occupied = pair_ref.shape
    width = sent_ref.shape[1]
    count = rows // occupied
    block = (occupied, rows)
    same = lax.broadcasted_iota(jnp.int32, block, 0) == lax.broadcasted_iota(jnp.int32, block, 1) % occupied
    picked = jnp.concatenate(
        [
            jnp.where(same, gram[n * occupied : (n + 1) * occupied], 0.0).sum(0, keepdims=True)
            for n in range(count)
        ]
    )
    owner = lax.broadcasted_iota(jnp.int32, (rows, width), 0) // occupied
    place = lax.broadcasted_iota(jnp.int32, (rows, width), 1)
    density = jnp.dot(
        picked,
        jnp.where(owner == place, 1.0, 0.0),
        precision=lax.Precision.HIGHEST,
        preferred_element_type=jnp.float32,
    )
    density = jnp.concatenate([density, jnp.zeros((16 - count, width), jnp.float32)])
    density_ref[...] = density
    put_parts(sent_ref, NZ * rows, density)


def middle(late, pieces, a, sums, stack, terms, pair_rows, coulomb, amp):
    rows, virtuals = sums.shape
    width = pieces[0].shape[1]
    return pl.pallas_call(
        functools.partial(middle_kernel, late),
        out_shape=(
            jax.ShapeDtypeStruct(stack.shape, stack.dtype),
            jax.ShapeDtypeStruct((rows, virtuals), jnp.bfloat16),
            jax.ShapeDtypeStruct((NZ * rows + 32, width), jnp.bfloat16),
            jax.ShapeDtypeStruct((16, width), jnp.float32),
        ),
        in_specs=[VMEM] * (8 + len(late)),
        out_specs=(VMEM,) * 4,
        scratch_shapes=[
            pltpu.VMEM((rows, virtuals), jnp.float32),
            pltpu.VMEM((rows, rows), jnp.float32),
        ],
        input_output_aliases={7 + len(late): 0},
        compiler_params=pltpu.CompilerParams(vmem_limit_bytes=VMEM_LIMIT),
    )(a, *pieces, sums, *terms, pair_rows, coulomb, amp, stack)


def kept_kernel(left_ref, stack_ref, out_ref):
    gamma_dots(0, left_ref[...], stack_ref, out_ref)


def gamma_kept(left, stack):
    rows, virtuals = left.shape
    width = stack.shape[2]
    return pl.pallas_call(
        kept_kernel,
        out_shape=jax.ShapeDtypeStruct((NZ * rows, width), jnp.float32),
        in_specs=[VMEM, VMEM],
        out_specs=VMEM,
        compiler_params=pltpu.CompilerParams(vmem_limit_bytes=SMALL_LIMIT),
        cost_estimate=pl.CostEstimate(
            flops=2 * rows * virtuals * width * NZ,
            bytes_accessed=2 * virtuals * width * NZ,
            transcendentals=0,
        ),
    )(left, stack)


def put_parts(ref, first, values):
    high = values.astype(jnp.bfloat16)
    ref[first : first + 16] = high
    ref[first + 16 : first + 32] = (values - high.astype(jnp.float32)).astype(jnp.bfloat16)


def wide(ref, first, rows):
    return ref[first : first + rows].astype(jnp.float32)


def got_parts(ref, first):
    return wide(ref, first, 16) + wide(ref, first + 16, 16)


def first_kernel(kept_ref, own_ref, recv_ref, mine_ref, one_ref, two_ref, three_ref, keep_ref, send_ref, out_ref):
    upper, lower = mine_ref.shape[0] // 2, keep_ref.shape[0] // NY
    rows = upper + lower
    for hi in range(2):
        for n, ref in enumerate((mine_ref, one_ref, two_ref, three_ref)):
            first = (hi * NY + n) * rows
            total = kept_ref[first : first + upper] + wide(recv_ref, first, upper)
            ref[hi * upper : (hi + 1) * upper] = total.astype(ref.dtype)
            first += upper
            total = kept_ref[first : first + lower] + wide(recv_ref, first, lower)
            ref = send_ref if hi else keep_ref
            ref[n * lower : (n + 1) * lower] = total.astype(ref.dtype)
    density = own_ref[...] + got_parts(recv_ref, NZ * rows)
    out_ref[...] = density
    put_parts(send_ref, NY * lower, density)


def first_sums(kept, density, received):
    rows, width = kept.shape[0] // NZ, kept.shape[1]
    upper, lower = UPPER, rows - UPPER
    shape = lambda n, kind: jax.ShapeDtypeStruct((n, width), kind)
    message = shape(2 * upper, jnp.bfloat16)
    return pl.pallas_call(
        first_kernel,
        out_shape=(
            shape(2 * upper, jnp.float32),
            message,
            message,
            message,
            shape(NY * lower, jnp.float32),
            shape(NY * lower + 32, jnp.bfloat16),
            shape(16, jnp.float32),
        ),
        in_specs=[VMEM] * 3,
        out_specs=(VMEM,) * 7,
        compiler_params=pltpu.CompilerParams(vmem_limit_bytes=SMALL_LIMIT),
    )(kept, density, received)


def to_owners(messages):
    one, two, three = messages
    two = along_y(two, 2)
    return along_y(one, 1), two, along_y(three, -1)


def second_kernel(
    mine_ref, a_ref, b_ref, c_ref, keep_ref, recv_ref, density_ref,
    upper_ref, send_ref, lower_ref, one_ref, two_ref, three_ref, out_ref,
):
    upper, lower = upper_ref.shape[0], lower_ref.shape[0]
    for hi, ref in enumerate((upper_ref, send_ref)):
        first = hi * upper
        arrived = sum(wide(other, first, upper) for other in (a_ref, b_ref, c_ref))
        ref[...] = (mine_ref[first : first + upper] + arrived).astype(ref.dtype)
    density = density_ref[...] + got_parts(recv_ref, NY * lower)
    out_ref[...] = density
    for n, ref in enumerate((lower_ref, one_ref, two_ref, three_ref)):
        first = n * lower
        total = keep_ref[first : first + lower] + wide(recv_ref, first, lower)
        ref[:lower] = total.astype(ref.dtype)
        if n:
            put_parts(ref, lower, density)


def second_sums(mine, arrived, keep, received, density):
    upper, lower, width = mine.shape[0] // 2, keep.shape[0] // NY, mine.shape[1]
    shape = lambda n, kind: jax.ShapeDtypeStruct((n, width), kind)
    message = shape(lower + 32, jnp.bfloat16)
    return pl.pallas_call(
        second_kernel,
        out_shape=(
            shape(upper, jnp.float32),
            shape(upper, jnp.bfloat16),
            shape(lower, jnp.float32),
            message,
            message,
            message,
            shape(16, jnp.float32),
        ),
        in_specs=[VMEM] * 7,
        out_specs=(VMEM,) * 7,
        compiler_params=pltpu.CompilerParams(vmem_limit_bytes=SMALL_LIMIT),
    )(mine, *arrived, keep, received, density)


def last_kernel(
    scale, upper_ref, recv_ref, lower_ref, a_ref, b_ref, c_ref, density_ref, gamma_ref, out_ref
):
    upper, lower = upper_ref.shape[0], lower_ref.shape[0]
    gamma_ref[:upper] = upper_ref[...] + wide(recv_ref, 0, upper)
    arrived = (a_ref, b_ref, c_ref)
    gamma_ref[upper:] = lower_ref[...] + sum(wide(ref, 0, lower) for ref in arrived)
    density = density_ref[...] + sum(got_parts(ref, lower) for ref in arrived)
    count = out_ref.shape[0]
    out_ref[...] = density[:count, :count] / scale


def last_sums(scale, count, upper, received, lower, arrived, density):
    rows, width = upper.shape[0] + lower.shape[0], upper.shape[1]
    return pl.pallas_call(
        functools.partial(last_kernel, scale),
        out_shape=(
            jax.ShapeDtypeStruct((rows, width), jnp.float32),
            jax.ShapeDtypeStruct((count, count), jnp.float32),
        ),
        in_specs=[VMEM] * 7,
        out_specs=(VMEM, VMEM),
        compiler_params=pltpu.CompilerParams(vmem_limit_bytes=SMALL_LIMIT),
    )(upper, received, lower, *arrived, density)


def body(
    b_vo, b_vv, amplitudes, pair_amps, coulomb_occ, eps_occ, eps_vir, c_index, a_index, b_index
):
    count_a, occupied, aux_all = b_vo.shape
    rows = count_a * occupied
    virtuals = b_vv.shape[1]
    pair_cols = amplitudes.shape[1]
    vo_rows = b_vo.reshape(rows, aux_all)
    tables = (a_index, b_index, c_index, eps_vir, eps_occ.reshape(1, occupied))
    late, pieces, sums, stack, terms, pair_rows, amp = gather_pieces(
        b_vv[0], amplitudes, pair_amps.reshape(rows, occupied), vo_rows, tables
    )
    stack, left, sent, density = middle(
        late, pieces, vo_rows, sums, stack, terms, pair_rows, coulomb_occ, amp
    )
    received = swap_core(sent)
    kept = gamma_kept(left, stack)
    mine, *messages, keep, send, density = first_sums(kept, density, received)
    arrived, received = together(to_owners(messages), swap_x_hi(send))
    upper, send, lower, *messages, density = second_sums(mine, arrived, keep, received, density)
    arrived, received = together(to_owners(messages), swap_x_hi(send))
    scale = lax.axis_size("ba") * occupied * occupied
    gamma, density = last_sums(scale, count_a, upper, received, lower, arrived, density)
    return gamma.reshape(count_a, occupied, gamma.shape[1]), density


def solution(mesh):
    placed = (
        P("aa", None, None),
        P("ba", None, "aa"),
        P("ba", None),
        P("aa", "ba", None),
        P(),
        P(),
        P(),
        P(),
        P("aa"),
        P("ba"),
    )
    return jax.shard_map(
        body,
        mesh=mesh,
        in_specs=placed,
        out_specs=(P("aa", None, "ba"), P("aa", None)),
        check_vma=False,
    )
```

```python
import functools

import jax
import jax.numpy as jnp
from jax import lax
from jax.experimental import pallas as pl
from jax.experimental.pallas import tpu as pltpu
from jax.sharding import PartitionSpec as P

NZ = 8
NY = 4
RANKS = 16
VMEM_LIMIT = 24 * 1024 * 1024
SMALL_LIMIT = 16 * 1024 * 1024
TILE = 768
UPPER = 160
NT = (((1,), (1,)), ((), ()))


def shift_perm(step):
    return [(i, (i + step) % RANKS) for i in range(RANKS)]


def swap_perm(bit):
    return [(i, i ^ bit) for i in range(RANKS)]


def along_z(x, step):
    return lax.ppermute(x, "aa", shift_perm(2 * step))


def swap_x_lo(x):
    return lax.ppermute(x, "aa", swap_perm(1))


def along_y(x, step):
    return lax.ppermute(x, "ba", shift_perm(4 * step))


def swap_x_hi(x):
    return lax.ppermute(x, "ba", swap_perm(2))


def swap_core(x):
    return lax.ppermute(x, "ba", swap_perm(1))


def together(*arrays):
    return lax.optimization_barrier(arrays)


VMEM = pl.BlockSpec(memory_space=pltpu.VMEM)
SMEM = pl.BlockSpec(memory_space=pltpu.SMEM)


def where_am_i():
    aa, ba = lax.axis_index("aa"), lax.axis_index("ba")
    z, x_lo = aa // 2, aa % 2
    y, x_hi, core = ba // 4, (ba // 2) % 2, ba % 2
    return z, x_lo, y, x_hi, core


def column_start(place, width):
    z, x_lo = where_am_i()[:2]
    column = (z + place % NZ) % NZ * 2 + (x_lo if place < NZ else 1 - x_lo)
    return pl.multiple_of(column * width, width)


def columns_of(a_ref, place, width):
    return a_ref[:, pl.ds(column_start(place, width), width)]


def terms_kernel(a_index_ref, b_index_ref, c_index_ref, table_ref, eps_ref, row_ref, col_ref):
    occupied = eps_ref.shape[1]
    along = lambda axis, shape: lax.broadcasted_iota(jnp.int32, shape, axis)
    square = (occupied, occupied)
    eps = jnp.sum(
        jnp.where(along(0, square) == along(1, square), eps_ref[...], 0.0), axis=1, keepdims=True
    )
    energy_b, energy_c = table_ref[b_index_ref[0]], table_ref[c_index_ref[0]]
    for n in range(a_index_ref.shape[0]):
        row_ref[n * occupied : (n + 1) * occupied] = (
            eps - table_ref[a_index_ref[n]] - energy_b - energy_c
        )
    wide = (occupied, col_ref.shape[1])
    picked = lambda labels: jnp.sum(
        jnp.where(along(0, wide) == labels, eps, 0.0), axis=0, keepdims=True
    )
    col_ref[...] = picked(along(1, wide) // occupied) + picked(along(1, wide) % occupied)


def energy_terms(tables):
    occupied = tables[-1].shape[1]
    return pl.pallas_call(
        terms_kernel,
        out_shape=(
            jax.ShapeDtypeStruct((tables[0].shape[0] * occupied, 1), jnp.float32),
            jax.ShapeDtypeStruct((1, occupied * occupied), jnp.float32),
        ),
        in_specs=[SMEM] * 4 + [VMEM],
        out_specs=(VMEM, VMEM),
        compiler_params=pltpu.CompilerParams(vmem_limit_bytes=SMALL_LIMIT),
    )(*tables)


def pack_kernel(*refs):
    for n, ref in enumerate(refs[:-1]):
        refs[-1][n] = ref[...]


def pack(arrays):
    return pl.pallas_call(
        pack_kernel,
        out_shape=jax.ShapeDtypeStruct((len(arrays), *arrays[0].shape), arrays[0].dtype),
        in_specs=[VMEM] * len(arrays),
        out_specs=VMEM,
        compiler_params=pltpu.CompilerParams(vmem_limit_bytes=SMALL_LIMIT),
    )(*arrays)


def whole_kernel(own_ref, other_ref, out_ref):
    _, _, y, x_hi, core = where_am_i()
    part = own_ref.shape[2]
    for other_core, ref in enumerate((own_ref, other_ref)):
        for n in range(NY):
            for other_hi in range(2):
                hi = 1 - x_hi if other_hi else x_hi
                owner = ((y + n) % NY * 2 + hi) * 2 + (1 - core if other_core else core)
                out_ref[pl.ds(pl.multiple_of(owner * part, part), part)] = ref[n, other_hi]


def whole_amplitudes(own, other):
    part, columns = own.shape[2:]
    return pl.pallas_call(
        whole_kernel,
        out_shape=jax.ShapeDtypeStruct((RANKS * part, columns), own.dtype),
        in_specs=[VMEM] * 2,
        out_specs=VMEM,
        compiler_params=pltpu.CompilerParams(vmem_limit_bytes=SMALL_LIMIT),
    )(own, other)


def add_kernel(places, first, a_ref, *refs):
    count = len(places)
    pieces, rest = refs[:count], refs[count:]
    if first:
        out_ref, stack_ref = rest
    else:
        before_ref, _, out_ref, stack_ref = rest
    for n, (place, piece) in enumerate(zip(places, pieces)):
        stack_ref[place] = piece[...]
        terms = lax.dot_general(
            columns_of(a_ref, place, piece.shape[1]),
            piece[...],
            NT,
            preferred_element_type=jnp.float32,
        )
        if n:
            out_ref[...] += terms
        else:
            out_ref[...] = terms if first else before_ref[...] + terms


def add_products(places, pieces, a, before=()):
    rows = a.shape[0]
    virtuals, width = pieces[0].shape
    count = len(pieces)
    return pl.pallas_call(
        functools.partial(add_kernel, places, not before),
        out_shape=(
            jax.ShapeDtypeStruct((rows, virtuals), jnp.float32),
            jax.ShapeDtypeStruct((2 * NZ, virtuals, width), pieces[0].dtype),
        ),
        in_specs=[VMEM] * (1 + count + len(before)),
        out_specs=(VMEM, VMEM),
        input_output_aliases={1 + count: 0, 2 + count: 1} if before else {},
        compiler_params=pltpu.CompilerParams(vmem_limit_bytes=VMEM_LIMIT),
        cost_estimate=pl.CostEstimate(
            flops=2 * rows * virtuals * width * count,
            bytes_accessed=2 * virtuals * width * count,
            transcendentals=0,
        ),
    )(a, *pieces, *before)


def gather_pieces(piece, amplitudes, pair_rows, a, tables):
    own, other = {0: piece}, {}
    get = lambda n: other[n - NZ] if n >= NZ else own[n]
    add = lambda places, **rest: add_products(places, [get(n) for n in places], a, **rest)
    own[7], own[1], other[0], amp_hi, terms, pair_rows, sums = together(
        along_z(piece, 1),
        along_z(piece, -1),
        swap_x_lo(piece),
        swap_x_hi(amplitudes),
        energy_terms(tables),
        pair_rows,
        add([0]),
    )
    amp = pack([amplitudes, amp_hi])
    sums = add([1, 7, NZ], before=sums)
    amp_up, amp_down = along_y(amp, -1), along_y(amp, 1)
    own[6], own[2], other[1], sums = together(
        along_z(own[7], 1), along_z(own[1], -1), swap_x_lo(own[1]), sums
    )
    sums = add([2, 6, NZ + 1], before=sums)
    own[5], own[3], other[7], sums, amp_up, amp_down = together(
        along_z(own[6], 1), along_z(own[2], -1), swap_x_lo(own[7]), sums, amp_up, amp_down
    )
    sums = add([3, 5, NZ + 7], before=sums)
    own[4], other[2], other[3], sums, amp_far = together(
        along_z(own[5], 1), along_z(other[1], -1), swap_x_lo(own[3]), sums, along_y(amp_up, -1)
    )
    amp_own = pack([amp, amp_up, amp_far, amp_down])
    amp_other = swap_core(amp_own)
    other[6], other[4], other[5] = (
        along_z(other[7], 1), along_z(other[3], -1), swap_x_lo(own[5])
    )
    sums, stack = add([4, NZ + 2, NZ + 3], before=sums)
    late = [NZ + 4, NZ + 5, NZ + 6]
    return late, [get(n) for n in late], sums, stack, terms, pair_rows, whole_amplitudes(amp_own, amp_other)


def gamma_dots(goes, left, stack_ref, out_ref):
    z, x_lo, y, x_hi, core = where_am_i()
    first = jnp.where(x_lo == core, goes, 1 - goes) * NZ
    rows = left.shape[0]
    for n in range(NZ):
        target = (y + n) % NY * 2 + (x_hi if n < NY else 1 - x_hi)
        out_ref[n * rows : (n + 1) * rows] = jnp.dot(
            left, stack_ref[first + (target - z + NZ) % NZ], preferred_element_type=jnp.float32
        ).astype(out_ref.dtype)


def middle_kernel(late, a_ref, *refs):
    count = len(late)
    pieces, (before_ref, row_ref, col_ref, pair_ref, coulomb_ref), rest = (
        refs[:count], refs[count : count + 5], refs[count + 5 :]
    )
    amp_ref, _, stack_ref, left_ref, sent_ref, density_ref, total, gram = rest
    products = before_ref[...]
    for place, piece in zip(late, pieces):
        stack_ref[place] = piece[...]
        products += lax.dot_general(
            columns_of(a_ref, place, piece.shape[1]),
            piece[...],
            NT,
            preferred_element_type=jnp.float32,
        )
    x = products.astype(jnp.bfloat16)

    tiles = [slice(n, n + TILE) for n in range(0, amp_ref.shape[1], TILE)]
    for n, tile in enumerate(tiles):
        triples = jnp.dot(
            x, amp_ref[:, tile], preferred_element_type=jnp.float32
        ) - jnp.dot(pair_ref[...], coulomb_ref[:, tile], preferred_element_type=jnp.float32)
        ratio = (triples / (row_ref[...] + col_ref[:, tile])).astype(jnp.bfloat16)
        terms = lax.dot_general(ratio, amp_ref[:, tile], NT, preferred_element_type=jnp.float32)
        pairs = lax.dot_general(ratio, ratio, NT, preferred_element_type=jnp.float32)
        if n == 0:
            total[...] = terms
            gram[...] = pairs
        else:
            total[...] += terms
            gram[...] += pairs
    left_ref[...] = total[...].astype(left_ref.dtype)

    gamma_dots(1, left_ref[...], stack_ref, sent_ref)

    rows, occupied = pair_ref.shape
    width = sent_ref.shape[1]
    count = rows // occupied
    block = (occupied, rows)
    same = lax.broadcasted_iota(jnp.int32, block, 0) == lax.broadcasted_iota(jnp.int32, block, 1) % occupied
    picked = jnp.concatenate(
        [
            jnp.where(same, gram[n * occupied : (n + 1) * occupied], 0.0).sum(0, keepdims=True)
            for n in range(count)
        ]
    )
    lane = lax.broadcasted_iota(jnp.int32, (count, rows), 1)
    place = lax.broadcasted_iota(jnp.int32, (count, width), 1)
    density = jnp.zeros((count, width), jnp.float32)
    for n in range(count):
        inside = jnp.logical_and(lane >= n * occupied, lane < (n + 1) * occupied)
        total_n = jnp.sum(jnp.where(inside, picked, 0.0), axis=1, keepdims=True)
        density = jnp.where(place == n, total_n, density)
    density = jnp.concatenate([density, jnp.zeros((16 - count, width), jnp.float32)])
    density_ref[...] = density
    put_parts(sent_ref, NZ * rows, density)


def middle(late, pieces, a, sums, stack, terms, pair_rows, coulomb, amp):
    rows, virtuals = sums.shape
    width = pieces[0].shape[1]
    return pl.pallas_call(
        functools.partial(middle_kernel, late),
        out_shape=(
            jax.ShapeDtypeStruct(stack.shape, stack.dtype),
            jax.ShapeDtypeStruct((rows, virtuals), jnp.bfloat16),
            jax.ShapeDtypeStruct((NZ * rows + 32, width), jnp.bfloat16),
            jax.ShapeDtypeStruct((16, width), jnp.float32),
        ),
        in_specs=[VMEM] * (8 + len(late)),
        out_specs=(VMEM,) * 4,
        scratch_shapes=[
            pltpu.VMEM((rows, virtuals), jnp.float32),
            pltpu.VMEM((rows, rows), jnp.float32),
        ],
        input_output_aliases={7 + len(late): 0},
        compiler_params=pltpu.CompilerParams(vmem_limit_bytes=VMEM_LIMIT),
    )(a, *pieces, sums, *terms, pair_rows, coulomb, amp, stack)


def kept_kernel(left_ref, stack_ref, out_ref):
    gamma_dots(0, left_ref[...], stack_ref, out_ref)


def gamma_kept(left, stack):
    rows, virtuals = left.shape
    width = stack.shape[2]
    return pl.pallas_call(
        kept_kernel,
        out_shape=jax.ShapeDtypeStruct((NZ * rows, width), jnp.float32),
        in_specs=[VMEM, VMEM],
        out_specs=VMEM,
        compiler_params=pltpu.CompilerParams(vmem_limit_bytes=SMALL_LIMIT),
        cost_estimate=pl.CostEstimate(
            flops=2 * rows * virtuals * width * NZ,
            bytes_accessed=2 * virtuals * width * NZ,
            transcendentals=0,
        ),
    )(left, stack)


def put_parts(ref, first, values):
    high = values.astype(jnp.bfloat16)
    ref[first : first + 16] = high
    ref[first + 16 : first + 32] = (values - high.astype(jnp.float32)).astype(jnp.bfloat16)


def wide(ref, first, rows):
    return ref[first : first + rows].astype(jnp.float32)


def got_parts(ref, first):
    return wide(ref, first, 16) + wide(ref, first + 16, 16)


def first_kernel(kept_ref, own_ref, recv_ref, mine_ref, one_ref, two_ref, three_ref, keep_ref, send_ref, out_ref):
    upper, lower = mine_ref.shape[0] // 2, keep_ref.shape[0] // NY
    rows = upper + lower
    for hi in range(2):
        for n, ref in enumerate((mine_ref, one_ref, two_ref, three_ref)):
            first = (hi * NY + n) * rows
            total = kept_ref[first : first + upper] + wide(recv_ref, first, upper)
            ref[hi * upper : (hi + 1) * upper] = total.astype(ref.dtype)
            first += upper
            total = kept_ref[first : first + lower] + wide(recv_ref, first, lower)
            ref = send_ref if hi else keep_ref
            ref[n * lower : (n + 1) * lower] = total.astype(ref.dtype)
    density = own_ref[...] + got_parts(recv_ref, NZ * rows)
    out_ref[...] = density
    put_parts(send_ref, NY * lower, density)


def first_sums(kept, density, received):
    rows, width = kept.shape[0] // NZ, kept.shape[1]
    upper, lower = UPPER, rows - UPPER
    shape = lambda n, kind: jax.ShapeDtypeStruct((n, width), kind)
    message = shape(2 * upper, jnp.bfloat16)
    return pl.pallas_call(
        first_kernel,
        out_shape=(
            shape(2 * upper, jnp.float32),
            message,
            message,
            message,
            shape(NY * lower, jnp.float32),
            shape(NY * lower + 32, jnp.bfloat16),
            shape(16, jnp.float32),
        ),
        in_specs=[VMEM] * 3,
        out_specs=(VMEM,) * 7,
        compiler_params=pltpu.CompilerParams(vmem_limit_bytes=SMALL_LIMIT),
    )(kept, density, received)


def to_owners(messages):
    one, two, three = messages
    two = along_y(two, 2)
    return along_y(one, 1), two, along_y(three, -1)


def second_kernel(
    mine_ref, a_ref, b_ref, c_ref, keep_ref, recv_ref, density_ref,
    upper_ref, send_ref, lower_ref, one_ref, two_ref, three_ref, out_ref,
):
    upper, lower = upper_ref.shape[0], lower_ref.shape[0]
    for hi, ref in enumerate((upper_ref, send_ref)):
        first = hi * upper
        arrived = sum(wide(other, first, upper) for other in (a_ref, b_ref, c_ref))
        ref[...] = (mine_ref[first : first + upper] + arrived).astype(ref.dtype)
    density = density_ref[...] + got_parts(recv_ref, NY * lower)
    out_ref[...] = density
    for n, ref in enumerate((lower_ref, one_ref, two_ref, three_ref)):
        first = n * lower
        total = keep_ref[first : first + lower] + wide(recv_ref, first, lower)
        ref[:lower] = total.astype(ref.dtype)
        if n:
            put_parts(ref, lower, density)


def second_sums(mine, arrived, keep, received, density):
    upper, lower, width = mine.shape[0] // 2, keep.shape[0] // NY, mine.shape[1]
    shape = lambda n, kind: jax.ShapeDtypeStruct((n, width), kind)
    message = shape(lower + 32, jnp.bfloat16)
    return pl.pallas_call(
        second_kernel,
        out_shape=(
            shape(upper, jnp.float32),
            shape(upper, jnp.bfloat16),
            shape(lower, jnp.float32),
            message,
            message,
            message,
            shape(16, jnp.float32),
        ),
        in_specs=[VMEM] * 7,
        out_specs=(VMEM,) * 7,
        compiler_params=pltpu.CompilerParams(vmem_limit_bytes=SMALL_LIMIT),
    )(mine, *arrived, keep, received, density)


def last_kernel(
    scale, upper_ref, recv_ref, lower_ref, a_ref, b_ref, c_ref, density_ref, gamma_ref, out_ref
):
    upper, lower = upper_ref.shape[0], lower_ref.shape[0]
    gamma_ref[:upper] = upper_ref[...] + wide(recv_ref, 0, upper)
    arrived = (a_ref, b_ref, c_ref)
    gamma_ref[upper:] = lower_ref[...] + sum(wide(ref, 0, lower) for ref in arrived)
    density = density_ref[...] + sum(got_parts(ref, lower) for ref in arrived)
    count = out_ref.shape[0]
    out_ref[...] = density[:count, :count] / scale


def last_sums(scale, count, upper, received, lower, arrived, density):
    rows, width = upper.shape[0] + lower.shape[0], upper.shape[1]
    return pl.pallas_call(
        functools.partial(last_kernel, scale),
        out_shape=(
            jax.ShapeDtypeStruct((rows, width), jnp.float32),
            jax.ShapeDtypeStruct((count, count), jnp.float32),
        ),
        in_specs=[VMEM] * 7,
        out_specs=(VMEM, VMEM),
        compiler_params=pltpu.CompilerParams(vmem_limit_bytes=SMALL_LIMIT),
    )(upper, received, lower, *arrived, density)


def body(
    b_vo, b_vv, amplitudes, pair_amps, coulomb_occ, eps_occ, eps_vir, c_index, a_index, b_index
):
    count_a, occupied, aux_all = b_vo.shape
    rows = count_a * occupied
    virtuals = b_vv.shape[1]
    pair_cols = amplitudes.shape[1]
    vo_rows = b_vo.reshape(rows, aux_all)
    tables = (a_index, b_index, c_index, eps_vir, eps_occ.reshape(1, occupied))
    late, pieces, sums, stack, terms, pair_rows, amp = gather_pieces(
        b_vv[0], amplitudes, pair_amps.reshape(rows, occupied), vo_rows, tables
    )
    stack, left, sent, density = middle(
        late, pieces, vo_rows, sums, stack, terms, pair_rows, coulomb_occ, amp
    )
    received = swap_core(sent)
    kept = gamma_kept(left, stack)
    mine, *messages, keep, send, density = first_sums(kept, density, received)
    arrived, received = together(to_owners(messages), swap_x_hi(send))
    upper, send, lower, *messages, density = second_sums(mine, arrived, keep, received, density)
    arrived, received = together(to_owners(messages), swap_x_hi(send))
    scale = lax.axis_size("ba") * occupied * occupied
    gamma, density = last_sums(scale, count_a, upper, received, lower, arrived, density)
    return gamma.reshape(count_a, occupied, gamma.shape[1]), density


def solution(mesh):
    placed = (
        P("aa", None, None),
        P("ba", None, "aa"),
        P("ba", None),
        P("aa", "ba", None),
        P(),
        P(),
        P(),
        P(),
        P("aa"),
        P("ba"),
    )
    return jax.shard_map(
        body,
        mesh=mesh,
        in_specs=placed,
        out_specs=(P("aa", None, "ba"), P("aa", None)),
        check_vma=False,
    )
```

```python
import functools

import jax
import jax.numpy as jnp
from jax import lax
from jax.experimental import pallas as pl
from jax.experimental.pallas import tpu as pltpu
from jax.sharding import PartitionSpec as P

NZ = 8
NY = 4
RANKS = 16
LANES = 128
VMEM_LIMIT = 24 * 1024 * 1024
SMALL_LIMIT = 16 * 1024 * 1024
TILE = 768
UPPER = 160
NT = (((1,), (1,)), ((), ()))


def shift_perm(step):
    return [(i, (i + step) % RANKS) for i in range(RANKS)]


def swap_perm(bit):
    return [(i, i ^ bit) for i in range(RANKS)]


def along_z(x, step):
    return lax.ppermute(x, "aa", shift_perm(2 * step))


def swap_x_lo(x):
    return lax.ppermute(x, "aa", swap_perm(1))


def along_y(x, step):
    return lax.ppermute(x, "ba", shift_perm(4 * step))


def swap_x_hi(x):
    return lax.ppermute(x, "ba", swap_perm(2))


def swap_core(x):
    return lax.ppermute(x, "ba", swap_perm(1))


def together(*arrays):
    return lax.optimization_barrier(arrays)


VMEM = pl.BlockSpec(memory_space=pltpu.VMEM)
SMEM = pl.BlockSpec(memory_space=pltpu.SMEM)


def where_am_i():
    aa, ba = lax.axis_index("aa"), lax.axis_index("ba")
    z, x_lo = aa // 2, aa % 2
    y, x_hi, core = ba // 4, (ba // 2) % 2, ba % 2
    return z, x_lo, y, x_hi, core


def column_start(place, width):
    z, x_lo = where_am_i()[:2]
    column = (z + place % NZ) % NZ * 2 + (x_lo if place < NZ else 1 - x_lo)
    return pl.multiple_of(column * width, width)


def columns_of(a_ref, place, width):
    return a_ref[:, pl.ds(column_start(place, width), width)]


def terms_kernel(a_index_ref, b_index_ref, c_index_ref, table_ref, eps_ref, row_ref, col_ref):
    occupied = eps_ref.shape[1]
    along = lambda axis, shape: lax.broadcasted_iota(jnp.int32, shape, axis)
    square = (occupied, occupied)
    eps = jnp.sum(
        jnp.where(along(0, square) == along(1, square), eps_ref[...], 0.0), axis=1, keepdims=True
    )
    energy_b, energy_c = table_ref[b_index_ref[0]], table_ref[c_index_ref[0]]
    for n in range(a_index_ref.shape[0]):
        row_ref[n * occupied : (n + 1) * occupied] = (
            eps - table_ref[a_index_ref[n]] - energy_b - energy_c
        )
    wide = (occupied, col_ref.shape[1])
    picked = lambda labels: jnp.sum(
        jnp.where(along(0, wide) == labels, eps, 0.0), axis=0, keepdims=True
    )
    col_ref[...] = picked(along(1, wide) // occupied) + picked(along(1, wide) % occupied)


def energy_terms(tables):
    occupied = tables[-1].shape[1]
    return pl.pallas_call(
        terms_kernel,
        out_shape=(
            jax.ShapeDtypeStruct((tables[0].shape[0] * occupied, 1), jnp.float32),
            jax.ShapeDtypeStruct((1, occupied * occupied), jnp.float32),
        ),
        in_specs=[SMEM] * 4 + [VMEM],
        out_specs=(VMEM, VMEM),
        compiler_params=pltpu.CompilerParams(vmem_limit_bytes=SMALL_LIMIT),
    )(*tables)


def pack_kernel(*refs):
    for n, ref in enumerate(refs[:-1]):
        refs[-1][n] = ref[...]


def pack(arrays):
    return pl.pallas_call(
        pack_kernel,
        out_shape=jax.ShapeDtypeStruct((len(arrays), *arrays[0].shape), arrays[0].dtype),
        in_specs=[VMEM] * len(arrays),
        out_specs=VMEM,
        compiler_params=pltpu.CompilerParams(vmem_limit_bytes=SMALL_LIMIT),
    )(*arrays)


def whole_kernel(own_ref, other_ref, coulomb_ref, out_ref):
    occupied, columns = coulomb_ref.shape
    first = out_ref.shape[0] - LANES
    out_ref[first : first + occupied] = coulomb_ref[...]
    out_ref[first + occupied :] = jnp.zeros((LANES - occupied, columns), out_ref.dtype)
    _, _, y, x_hi, core = where_am_i()
    part = own_ref.shape[2]
    for other_core, ref in enumerate((own_ref, other_ref)):
        for n in range(NY):
            for other_hi in range(2):
                hi = 1 - x_hi if other_hi else x_hi
                owner = ((y + n) % NY * 2 + hi) * 2 + (1 - core if other_core else core)
                out_ref[pl.ds(pl.multiple_of(owner * part, part), part)] = ref[n, other_hi]


def whole_amplitudes(own, other, coulomb):
    part, columns = own.shape[2:]
    return pl.pallas_call(
        whole_kernel,
        out_shape=jax.ShapeDtypeStruct((RANKS * part + LANES, columns), own.dtype),
        in_specs=[VMEM] * 3,
        out_specs=VMEM,
        compiler_params=pltpu.CompilerParams(vmem_limit_bytes=SMALL_LIMIT),
    )(own, other, coulomb)


def add_kernel(places, first, a_ref, *refs):
    count = len(places)
    pieces, rest = refs[:count], refs[count:]
    if first:
        out_ref, stack_ref = rest
    else:
        before_ref, _, out_ref, stack_ref = rest
    for n, (place, piece) in enumerate(zip(places, pieces)):
        stack_ref[place] = piece[...]
        terms = lax.dot_general(
            columns_of(a_ref, place, piece.shape[1]),
            piece[...],
            NT,
            preferred_element_type=jnp.float32,
        )
        if n:
            out_ref[...] += terms
        else:
            out_ref[...] = terms if first else before_ref[...] + terms


def add_products(places, pieces, a, before=()):
    rows = a.shape[0]
    virtuals, width = pieces[0].shape
    count = len(pieces)
    return pl.pallas_call(
        functools.partial(add_kernel, places, not before),
        out_shape=(
            jax.ShapeDtypeStruct((rows, virtuals), jnp.float32),
            jax.ShapeDtypeStruct((2 * NZ, virtuals, width), pieces[0].dtype),
        ),
        in_specs=[VMEM] * (1 + count + len(before)),
        out_specs=(VMEM, VMEM),
        input_output_aliases={1 + count: 0, 2 + count: 1} if before else {},
        compiler_params=pltpu.CompilerParams(vmem_limit_bytes=VMEM_LIMIT),
        cost_estimate=pl.CostEstimate(
            flops=2 * rows * virtuals * width * count,
            bytes_accessed=2 * virtuals * width * count,
            transcendentals=0,
        ),
    )(a, *pieces, *before)


def gather_pieces(piece, amplitudes, pair_rows, coulomb, a, tables):
    own, other = {0: piece}, {}
    get = lambda n: other[n - NZ] if n >= NZ else own[n]
    add = lambda places, **rest: add_products(places, [get(n) for n in places], a, **rest)
    own[7], own[1], other[0], amp_hi, terms, pair_rows, sums = together(
        along_z(piece, 1),
        along_z(piece, -1),
        swap_x_lo(piece),
        swap_x_hi(amplitudes),
        energy_terms(tables),
        pair_rows,
        add([0]),
    )
    amp = pack([amplitudes, amp_hi])
    sums = add([1, 7, NZ], before=sums)
    amp_up, amp_down = along_y(amp, -1), along_y(amp, 1)
    own[6], own[2], other[1], sums = together(
        along_z(own[7], 1), along_z(own[1], -1), swap_x_lo(own[1]), sums
    )
    sums = add([2, 6, NZ + 1], before=sums)
    own[5], own[3], other[7], sums, amp_up, amp_down = together(
        along_z(own[6], 1), along_z(own[2], -1), swap_x_lo(own[7]), sums, amp_up, amp_down
    )
    sums = add([3, 5, NZ + 7], before=sums)
    own[4], other[2], other[3], sums, amp_far = together(
        along_z(own[5], 1), along_z(other[1], -1), swap_x_lo(own[3]), sums, along_y(amp_up, -1)
    )
    amp_own = pack([amp, amp_up, amp_far, amp_down])
    amp_other = swap_core(amp_own)
    other[6], other[4], other[5] = (
        along_z(other[7], 1), along_z(other[3], -1), swap_x_lo(own[5])
    )
    sums, stack = add([4, NZ + 2, NZ + 3], before=sums)
    late = [NZ + 4, NZ + 5, NZ + 6]
    return late, [get(n) for n in late], sums, stack, terms, pair_rows, whole_amplitudes(amp_own, amp_other, coulomb)


def gamma_dots(goes, left, stack_ref, out_ref):
    z, x_lo, y, x_hi, core = where_am_i()
    first = jnp.where(x_lo == core, goes, 1 - goes) * NZ
    rows = left.shape[0]
    for n in range(NZ):
        target = (y + n) % NY * 2 + (x_hi if n < NY else 1 - x_hi)
        out_ref[n * rows : (n + 1) * rows] = jnp.dot(
            left, stack_ref[first + (target - z + NZ) % NZ], preferred_element_type=jnp.float32
        ).astype(out_ref.dtype)


def middle_kernel(late, a_ref, *refs):
    count = len(late)
    pieces, (before_ref, row_ref, col_ref, pair_ref), rest = (
        refs[:count], refs[count : count + 4], refs[count + 4 :]
    )
    amp_ref, _, stack_ref, left_ref, sent_ref, density_ref, x_ref, total, gram = rest
    products = before_ref[...]
    for place, piece in zip(late, pieces):
        stack_ref[place] = piece[...]
        products += lax.dot_general(
            columns_of(a_ref, place, piece.shape[1]),
            piece[...],
            NT,
            preferred_element_type=jnp.float32,
        )
    virtuals = products.shape[1]
    x_ref[:, :virtuals] = products.astype(jnp.bfloat16)
    x_ref[:, virtuals:] = jnp.zeros((x_ref.shape[0], LANES), jnp.bfloat16)
    x_ref[:, virtuals : virtuals + pair_ref.shape[1]] = -pair_ref[...]

    tiles = [slice(n, n + TILE) for n in range(0, amp_ref.shape[1], TILE)]
    for n, tile in enumerate(tiles):
        triples = jnp.dot(x_ref[...], amp_ref[:, tile], preferred_element_type=jnp.float32)
        ratio = (triples / (row_ref[...] + col_ref[:, tile])).astype(jnp.bfloat16)
        terms = lax.dot_general(ratio, amp_ref[:virtuals, tile], NT, preferred_element_type=jnp.float32)
        pairs = lax.dot_general(ratio, ratio, NT, preferred_element_type=jnp.float32)
        if n == 0:
            total[...] = terms
            gram[...] = pairs
        else:
            total[...] += terms
            gram[...] += pairs
    left_ref[...] = total[...].astype(left_ref.dtype)

    gamma_dots(1, left_ref[...], stack_ref, sent_ref)

    rows, occupied = pair_ref.shape
    width = sent_ref.shape[1]
    count = rows // occupied
    block = (occupied, rows)
    same = lax.broadcasted_iota(jnp.int32, block, 0) == lax.broadcasted_iota(jnp.int32, block, 1) % occupied
    picked = jnp.concatenate(
        [
            jnp.where(same, gram[n * occupied : (n + 1) * occupied], 0.0).sum(0, keepdims=True)
            for n in range(count)
        ]
    )
    lane = lax.broadcasted_iota(jnp.int32, (count, rows), 1)
    place = lax.broadcasted_iota(jnp.int32, (count, width), 1)
    density = jnp.zeros((count, width), jnp.float32)
    for n in range(count):
        inside = jnp.logical_and(lane >= n * occupied, lane < (n + 1) * occupied)
        total_n = jnp.sum(jnp.where(inside, picked, 0.0), axis=1, keepdims=True)
        density = jnp.where(place == n, total_n, density)
    density = jnp.concatenate([density, jnp.zeros((16 - count, width), jnp.float32)])
    density_ref[...] = density
    put_parts(sent_ref, NZ * rows, density)


def middle(late, pieces, a, sums, stack, terms, pair_rows, amp):
    rows, virtuals = sums.shape
    width = pieces[0].shape[1]
    return pl.pallas_call(
        functools.partial(middle_kernel, late),
        out_shape=(
            jax.ShapeDtypeStruct(stack.shape, stack.dtype),
            jax.ShapeDtypeStruct((rows, virtuals), jnp.bfloat16),
            jax.ShapeDtypeStruct((NZ * rows + 32, width), jnp.bfloat16),
            jax.ShapeDtypeStruct((16, width), jnp.float32),
        ),
        in_specs=[VMEM] * (7 + len(late)),
        out_specs=(VMEM,) * 4,
        scratch_shapes=[
            pltpu.VMEM((rows, virtuals + LANES), jnp.bfloat16),
            pltpu.VMEM((rows, virtuals), jnp.float32),
            pltpu.VMEM((rows, rows), jnp.float32),
        ],
        input_output_aliases={6 + len(late): 0},
        compiler_params=pltpu.CompilerParams(vmem_limit_bytes=VMEM_LIMIT),
    )(a, *pieces, sums, *terms, pair_rows, amp, stack)


def kept_kernel(left_ref, stack_ref, out_ref):
    gamma_dots(0, left_ref[...], stack_ref, out_ref)


def gamma_kept(left, stack):
    rows, virtuals = left.shape
    width = stack.shape[2]
    return pl.pallas_call(
        kept_kernel,
        out_shape=jax.ShapeDtypeStruct((NZ * rows, width), jnp.float32),
        in_specs=[VMEM, VMEM],
        out_specs=VMEM,
        compiler_params=pltpu.CompilerParams(vmem_limit_bytes=SMALL_LIMIT),
        cost_estimate=pl.CostEstimate(
            flops=2 * rows * virtuals * width * NZ,
            bytes_accessed=2 * virtuals * width * NZ,
            transcendentals=0,
        ),
    )(left, stack)


def put_parts(ref, first, values):
    high = values.astype(jnp.bfloat16)
    ref[first : first + 16] = high
    ref[first + 16 : first + 32] = (values - high.astype(jnp.float32)).astype(jnp.bfloat16)


def wide(ref, first, rows):
    return ref[first : first + rows].astype(jnp.float32)


def got_parts(ref, first):
    return wide(ref, first, 16) + wide(ref, first + 16, 16)


def first_kernel(kept_ref, own_ref, recv_ref, mine_ref, one_ref, two_ref, three_ref, keep_ref, send_ref, out_ref):
    upper, lower = mine_ref.shape[0] // 2, keep_ref.shape[0] // NY
    rows = upper + lower
    for hi in range(2):
        for n, ref in enumerate((mine_ref, one_ref, two_ref, three_ref)):
            first = (hi * NY + n) * rows
            total = kept_ref[first : first + upper] + wide(recv_ref, first, upper)
            ref[hi * upper : (hi + 1) * upper] = total.astype(ref.dtype)
            first += upper
            total = kept_ref[first : first + lower] + wide(recv_ref, first, lower)
            ref = send_ref if hi else keep_ref
            ref[n * lower : (n + 1) * lower] = total.astype(ref.dtype)
    density = own_ref[...] + got_parts(recv_ref, NZ * rows)
    out_ref[...] = density
    put_parts(send_ref, NY * lower, density)


def first_sums(kept, density, received):
    rows, width = kept.shape[0] // NZ, kept.shape[1]
    upper, lower = UPPER, rows - UPPER
    shape = lambda n, kind: jax.ShapeDtypeStruct((n, width), kind)
    message = shape(2 * upper, jnp.bfloat16)
    return pl.pallas_call(
        first_kernel,
        out_shape=(
            shape(2 * upper, jnp.float32),
            message,
            message,
            message,
            shape(NY * lower, jnp.float32),
            shape(NY * lower + 32, jnp.bfloat16),
            shape(16, jnp.float32),
        ),
        in_specs=[VMEM] * 3,
        out_specs=(VMEM,) * 7,
        compiler_params=pltpu.CompilerParams(vmem_limit_bytes=SMALL_LIMIT),
    )(kept, density, received)


def to_owners(messages):
    one, two, three = messages
    two = along_y(two, 2)
    return along_y(one, 1), two, along_y(three, -1)


def second_kernel(
    mine_ref, a_ref, b_ref, c_ref, keep_ref, recv_ref, density_ref,
    upper_ref, send_ref, lower_ref, one_ref, two_ref, three_ref, out_ref,
):
    upper, lower = upper_ref.shape[0], lower_ref.shape[0]
    for hi, ref in enumerate((upper_ref, send_ref)):
        first = hi * upper
        arrived = sum(wide(other, first, upper) for other in (a_ref, b_ref, c_ref))
        ref[...] = (mine_ref[first : first + upper] + arrived).astype(ref.dtype)
    density = density_ref[...] + got_parts(recv_ref, NY * lower)
    out_ref[...] = density
    for n, ref in enumerate((lower_ref, one_ref, two_ref, three_ref)):
        first = n * lower
        total = keep_ref[first : first + lower] + wide(recv_ref, first, lower)
        ref[:lower] = total.astype(ref.dtype)
        if n:
            put_parts(ref, lower, density)


def second_sums(mine, arrived, keep, received, density):
    upper, lower, width = mine.shape[0] // 2, keep.shape[0] // NY, mine.shape[1]
    shape = lambda n, kind: jax.ShapeDtypeStruct((n, width), kind)
    message = shape(lower + 32, jnp.bfloat16)
    return pl.pallas_call(
        second_kernel,
        out_shape=(
            shape(upper, jnp.float32),
            shape(upper, jnp.bfloat16),
            shape(lower, jnp.float32),
            message,
            message,
            message,
            shape(16, jnp.float32),
        ),
        in_specs=[VMEM] * 7,
        out_specs=(VMEM,) * 7,
        compiler_params=pltpu.CompilerParams(vmem_limit_bytes=SMALL_LIMIT),
    )(mine, *arrived, keep, received, density)


def last_kernel(
    scale, upper_ref, recv_ref, lower_ref, a_ref, b_ref, c_ref, density_ref, gamma_ref, out_ref
):
    upper, lower = upper_ref.shape[0], lower_ref.shape[0]
    gamma_ref[:upper] = upper_ref[...] + wide(recv_ref, 0, upper)
    arrived = (a_ref, b_ref, c_ref)
    gamma_ref[upper:] = lower_ref[...] + sum(wide(ref, 0, lower) for ref in arrived)
    density = density_ref[...] + sum(got_parts(ref, lower) for ref in arrived)
    count = out_ref.shape[0]
    out_ref[...] = density[:count, :count] / scale


def last_sums(scale, count, upper, received, lower, arrived, density):
    rows, width = upper.shape[0] + lower.shape[0], upper.shape[1]
    return pl.pallas_call(
        functools.partial(last_kernel, scale),
        out_shape=(
            jax.ShapeDtypeStruct((rows, width), jnp.float32),
            jax.ShapeDtypeStruct((count, count), jnp.float32),
        ),
        in_specs=[VMEM] * 7,
        out_specs=(VMEM, VMEM),
        compiler_params=pltpu.CompilerParams(vmem_limit_bytes=SMALL_LIMIT),
    )(upper, received, lower, *arrived, density)


def body(
    b_vo, b_vv, amplitudes, pair_amps, coulomb_occ, eps_occ, eps_vir, c_index, a_index, b_index
):
    count_a, occupied, aux_all = b_vo.shape
    rows = count_a * occupied
    virtuals = b_vv.shape[1]
    pair_cols = amplitudes.shape[1]
    vo_rows = b_vo.reshape(rows, aux_all)
    tables = (a_index, b_index, c_index, eps_vir, eps_occ.reshape(1, occupied))
    late, pieces, sums, stack, terms, pair_rows, amp = gather_pieces(
        b_vv[0], amplitudes, pair_amps.reshape(rows, occupied), coulomb_occ, vo_rows, tables
    )
    stack, left, sent, density = middle(
        late, pieces, vo_rows, sums, stack, terms, pair_rows, amp
    )
    received = swap_core(sent)
    kept = gamma_kept(left, stack)
    mine, *messages, keep, send, density = first_sums(kept, density, received)
    arrived, received = together(to_owners(messages), swap_x_hi(send))
    upper, send, lower, *messages, density = second_sums(mine, arrived, keep, received, density)
    arrived, received = together(to_owners(messages), swap_x_hi(send))
    scale = lax.axis_size("ba") * occupied * occupied
    gamma, density = last_sums(scale, count_a, upper, received, lower, arrived, density)
    return gamma.reshape(count_a, occupied, gamma.shape[1]), density


def solution(mesh):
    placed = (
        P("aa", None, None),
        P("ba", None, "aa"),
        P("ba", None),
        P("aa", "ba", None),
        P(),
        P(),
        P(),
        P(),
        P("aa"),
        P("ba"),
    )
    return jax.shard_map(
        body,
        mesh=mesh,
        in_specs=placed,
        out_specs=(P("aa", None, "ba"), P("aa", None)),
        check_vma=False,
    )
```
